32 devices in a mesh: slab: 8 (over z, y), mode: 4 (over x, core).
Axes of the slice: x: 2, y: 2, z: 4, core: 2. Of those that a mesh axis runs over, the one named last changes fastest.
Arguments:
- positions: float32 [3, 65536], P(None, ('slab', 'mode')), may hold values from 0 to 1, as said below
- charges: float32 [65536], P(('slab', 'mode')), may hold values from -0.0546875 to 0.0546875
- counts: int32 [8], replicated, may hold values from 1792 to 8192, as said below
- box: float32 [2], replicated, may hold values from 0.8 to 1.25
Outputs:
- forces: float32 [3, 65536], P(None, ('slab', 'mode'))
The draws below stay inside these ranges and needn't reach their ends.
Inputs may be any that keep to these rules, and one draw needn't show every extreme that they name: positions[0] and positions[1] are fractional coordinates; positions[2, i] lies strictly between s 0.08 / 8 and (s + 1) 0.08 / 8 for s = i // 8192, and never falls with i within a slab. The live ions of a slab are its first counts[s] slots; some slab is full.
All inputs are finite; a program needn't handle non-finite values.
Results may differ from the reference program's by a relative error of at most 0.0003.
Values sent between devices are 32-bit elements; how exact they have to be, the bound alone decides.
No kernel may reach another device: no remote copies, remote signals or barrier semaphores. Data moves between devices by JAX's collectives and lax.ppermute only.
A program may use at most 64 MiB of HBM per device.

```python
import math
import jax
import jax.numpy as jnp
from jax import lax

QDIM = 64
BLOCK = 512
MODES = 4096
ION_SLAB = 8192
IONS = 65536
N_SLAB = 8


slab_span = 0.08


def run_levels(key, run_width, spread):
    step_total = ION_SLAB + 1
    run_count = (step_total + run_width - 1) // run_width
    levels = jnp.exp(jax.random.uniform(key, (N_SLAB, run_count), jnp.float32, -spread, spread))
    run_index = jnp.arange(step_total, dtype=jnp.int32) // run_width
    return levels[:, run_index]


def draw_positions(key, part):
    keys = jax.random.split(jax.random.fold_in(key, 11), 5)
    frac_x = jax.random.uniform(keys[0], (N_SLAB * ION_SLAB,), jnp.float32)
    frac_y = jax.random.uniform(keys[1], (N_SLAB * ION_SLAB,), jnp.float32)
    base_steps = jax.random.uniform(keys[2], (N_SLAB, ION_SLAB + 1), jnp.float32, 0.2, 1.8)
    short_levels = run_levels(keys[3], max(1, BLOCK // 8), 2.0)
    long_levels = run_levels(keys[4], 2 * BLOCK, 4.0)
    steps_up = base_steps * short_levels * long_levels
    running = jnp.cumsum(steps_up, axis=1)
    fraction = running[:, :-1] / running[:, -1:]
    height = slab_span / N_SLAB
    heights = (jnp.arange(N_SLAB, dtype=jnp.float32)[:, None] + 0.001 + 0.998 * fraction) * height
    return jnp.stack([frac_x, frac_y, heights.reshape(-1)]).astype(jnp.float32)


def draw_counts(key, part):
    keys = jax.random.split(jax.random.fold_in(key, 23), 3)
    divisor = jax.random.randint(keys[0], (N_SLAB,), 1, 5)
    jitter = jax.random.randint(keys[1], (N_SLAB,), 0, BLOCK // 2 + 1)
    ragged = ION_SLAB // divisor - jitter
    full_slab = jax.random.randint(keys[2], (), 0, N_SLAB)
    return jnp.where(jnp.arange(N_SLAB) == full_slab, ION_SLAB, ragged).astype(jnp.int32)


def block_scale(rng, dims, shards, smallest, top_value):
    level, own = 1.0, jax.random.fold_in(rng, 6)
    for dim, parts in shards:
        draws = jnp.exp(jax.random.uniform(jax.random.fold_in(own, dim), (parts,), jnp.float32, smallest / len(shards), top_value / len(shards)))
        level = level * jnp.repeat(draws, dims[dim] // parts).reshape([-1 if axis == dim else 1 for axis in range(len(dims))])
    return level


def noise(key, shape, deviation, bound, cuts=(), kind=jnp.bfloat16):
    values = deviation * jax.random.normal(key, shape, jnp.float32)
    if cuts:
        values = values * block_scale(key, shape, cuts, -0.22, 0.18)
    return jnp.clip(values, -bound, bound).astype(kind)


def setup_inputs(seed: int = 0) -> dict:
    seeds = jax.random.split(jax.random.key(seed), 5)
    positions = draw_positions(jax.random.fold_in(seeds[4], 71), 0)
    charges = noise(seeds[1], (IONS,), (0.45 * (IONS * MODES) ** -0.25), 0.0546875, ((0, 32),), jnp.float32)
    counts = draw_counts(jax.random.fold_in(seeds[4], 71), 0)
    box = jnp.clip(jnp.exp(jax.random.uniform(seeds[3], (2,), jnp.float32, math.log(0.8), math.log(1.25))), 0.8, 1.25)
    return dict(positions=positions, charges=charges, counts=counts, box=box)


two_pi = 2.0 * math.pi
slab_span = 0.08

def wave_table(first_mode, mode_count, box):
    mode_index = first_mode + jnp.arange(mode_count, dtype=jnp.int32)
    order_p = (mode_index // QDIM + 1).astype(jnp.float32)
    order_q = (mode_index % QDIM - QDIM // 2).astype(jnp.float32)
    wave_x = two_pi * order_p / box[0]
    wave_y = two_pi * order_q / box[1]
    wave_norm = jnp.sqrt(wave_x * wave_x + wave_y * wave_y)
    return (order_p, order_q, wave_x / wave_norm, wave_y / wave_norm, wave_norm)

def phase_terms(mode_info, coords, lower_edge, height):
    order_p, order_q, unit_x, unit_y, wave_norm = mode_info
    phase_angle = two_pi * (order_p[:, None] * coords[0][None, :] + order_q[:, None] * coords[1][None, :])
    ion_depth = coords[2][None, :] - lower_edge
    e_low = jnp.exp(-wave_norm[:, None] * ion_depth)
    e_high = jnp.exp(-wave_norm[:, None] * (height - ion_depth))
    return (jnp.cos(phase_angle), jnp.sin(phase_angle), e_low, e_high)

def force_terms(mode_info, coords, weight, coefficients, lower_edge, height, box):
    order_p, order_q, unit_x, unit_y, wave_norm = mode_info
    cosine, sine_part, e_low, e_high = phase_terms(mode_info, coords, lower_edge, height)
    mode_count, ion_count = cosine.shape
    block_count = coefficients.shape[2]

    def spread(row_values):
        return jnp.broadcast_to(row_values[:, :, None], (mode_count, block_count, BLOCK)).reshape(mode_count, ion_count)
    below_c = e_low * spread(coefficients[0])
    below_s = e_low * spread(coefficients[1])
    above_c = e_high * spread(coefficients[2])
    above_s = e_high * spread(coefficients[3])
    in_plane = sine_part * (below_c + above_c) - cosine * (below_s + above_s)
    normal = cosine * (below_c - above_c) + sine_part * (below_s - above_s)
    scale = 2.0 * two_pi / (box[0] * box[1]) * weight
    return jnp.stack([lax.optimization_barrier(jnp.sum(unit_x[:, None] * in_plane, axis=0)), lax.optimization_barrier(jnp.sum(unit_y[:, None] * in_plane, axis=0)), lax.optimization_barrier(jnp.sum(normal, axis=0))]) * scale[None, :]

def reference(positions, charges, counts, box):
    height = slab_span / N_SLAB
    coords = positions.reshape(3, N_SLAB, ION_SLAB).transpose(1, 0, 2)
    charge = charges.reshape(N_SLAB, ION_SLAB)
    live_mask = jnp.arange(ION_SLAB, dtype=jnp.int32)[None, :] < counts[:, None]
    weight = jnp.where(live_mask, charge, jnp.float32(0.0))
    lower_edges = jnp.arange(N_SLAB, dtype=jnp.int32).astype(jnp.float32) * height
    group_size = 256 if MODES % 256 == 0 else MODES
    first_modes = jnp.arange(MODES // group_size, dtype=jnp.int32) * group_size
    block_count = ION_SLAB // BLOCK

    def slab_moments(slab_item):
        ion_place, ion_weight, lower_edge = slab_item

        def per_group(first_mode):
            mode_info = wave_table(first_mode, group_size, box)
            cosine, sine_part, e_low, e_high = phase_terms(mode_info, ion_place, lower_edge, height)
            upward = ion_weight[None, :] * e_high
            downward = ion_weight[None, :] * e_low
            row_stack = jnp.stack([upward * cosine, upward * sine_part, downward * cosine, downward * sine_part])
            return lax.optimization_barrier(jnp.sum(row_stack.reshape(4, group_size, block_count, BLOCK), axis=3))
        pieces = lax.map(per_group, first_modes)
        return pieces.transpose(1, 0, 2, 3).reshape(4, MODES, block_count)
    moments = lax.map(slab_moments, (coords, weight, lower_edges))
    wave_norm = wave_table(jnp.int32(0), MODES, box)[4]
    decay_step = jnp.exp(-wave_norm * height)
    totals = lax.optimization_barrier(jnp.sum(moments, axis=3))

    def advance(carried, total_here):
        return (decay_step[None, :] * carried + total_here, carried)
    zero_carry = jnp.zeros((2, MODES), jnp.float32)
    _, carry_up = lax.scan(advance, zero_carry, totals[:, 0:2])
    _, carry_down = lax.scan(advance, zero_carry, totals[:, 2:4], reverse=True)
    boost_step = jnp.exp(wave_norm * height)[None, None, :, None]
    prefix_up = jnp.cumsum(moments[:, 0:2], axis=3) - moments[:, 0:2]
    suffix_down = jnp.flip(jnp.cumsum(jnp.flip(moments[:, 2:4], 3), axis=3), 3) - moments[:, 2:4]
    coefficients = jnp.concatenate([carry_up[..., None] + boost_step * prefix_up, carry_down[..., None] + boost_step * suffix_down], axis=1)

    def slab_forces(slab_item):
        ion_place, ion_weight, lower_edge, coeff_table = slab_item

        def per_group(total_force, first_mode):
            mode_info = wave_table(first_mode, group_size, box)
            coeff_part = lax.dynamic_slice_in_dim(coeff_table, first_mode.astype(jnp.int32), group_size, 1)
            return (total_force + force_terms(mode_info, ion_place, ion_weight, coeff_part, lower_edge, height, box), None)
        total_force, _ = lax.scan(per_group, jnp.zeros((3, ION_SLAB), jnp.float32), first_modes)
        return total_force
    forces = lax.map(slab_forces, (coords, weight, lower_edges, coefficients))
    return forces.transpose(1, 0, 2).reshape(3, IONS)
```

```python
import functools
import math

import jax
import jax.numpy as jnp
import numpy as np
from jax import lax
from jax.experimental import pallas as pl
from jax.experimental.pallas import tpu as pltpu
from jax.sharding import PartitionSpec as P

QDIM = 64
BLOCK = 512
MODES = 4096
PDIM = MODES // QDIM
HALF = QDIM // 2
LANES = 4 * HALF

two_pi = 2.0 * math.pi
slab_span = 0.08
box_low = 0.8

SIN_TERMS = (3.14159264, -5.16771008, 2.55007752, -0.59829129, 0.07765766)
COS_TERMS = (1.0, -4.93480214, 4.05870916, -1.335212, 0.23493731, -0.02439632)


def series_terms(height):
    a = 0.5 * height * two_pi * math.hypot(PDIM, HALF) / box_low
    nodes = np.cos(np.pi * (np.arange(64) + 0.5) / 64)
    order = np.arange(32)[:, None]
    coefficients = np.abs((np.exp(-a * (1.0 + nodes)) * np.cos(order * np.arccos(nodes))).sum(1) / 32.0)
    count = 4
    while coefficients[count:].sum() > 2.0**-24:
        count += 4
    return count


def poly(terms, u):
    value = jnp.full_like(u, terms[-1])
    for term in terms[-2::-1]:
        value = value * u + term
    return value


def turn(angle):
    r = angle - jnp.floor(angle + 0.5)
    u = r * r
    s = r * poly(SIN_TERMS, u)
    c = poly(COS_TERMS, u)
    return 1.0 - 2.0 * s * s, 2.0 * s * c


def split(x):
    high = x.astype(jnp.bfloat16)
    return high, (x - high.astype(jnp.float32)).astype(jnp.bfloat16)


def iota(shape, dim):
    return lax.broadcasted_iota(jnp.int32, shape, dim)


def roll(x, shift):
    return pltpu.roll(x, shift % LANES, x.ndim - 1)


def even_group(shape):
    return (iota(shape, 1) // HALF) % 2 == 0


def swap_groups(x):
    return jnp.where(even_group(x.shape), roll(x, -HALF), roll(x, HALF))


def half_sign(shape):
    return jnp.where(iota(shape, 1) < LANES // 2, -1.0, 1.0)


def wave(order_p, order_q, box_x, box_y):
    wave_x = two_pi * order_p / box_x
    wave_y = two_pi * order_q / box_y
    return wave_x, wave_y, jnp.sqrt(wave_x * wave_x + wave_y * wave_y)


def tile_orders():
    shape = (PDIM, LANES)
    p = (iota(shape, 0) + 1).astype(jnp.float32)
    j = iota(shape, 1) % HALF
    return p, j.astype(jnp.float32), (-1 - j).astype(jnp.float32)


def table_terms(count, height, box_x, box_y):
    p, q_plus, q_minus = tile_orders()
    even = even_group(p.shape)
    a = (0.5 * height) * wave(p, jnp.where(even, q_plus, q_minus), box_x, box_y)[2]
    ratio = jnp.zeros_like(a)
    ratios = {}
    for n in range(count + 6, 0, -1):
        ratio = a / (2.0 * n + a * ratio)
        ratios[n] = ratio
    products = [jnp.ones_like(a)]
    total = jnp.ones_like(a)
    for n in range(1, count + 7):
        products.append(products[-1] * ratios[n])
        total = total + 2.0 * products[n]
    first = 1.0 / total
    terms = [first] + [(2.0 * first) * products[n] for n in range(1, count)]
    plus, minus = [], []
    for m in range(count // 2):
        low, high = terms[2 * m], terms[2 * m + 1]
        plus.append(jnp.where(even, low, roll(high, HALF)))
        minus.append(jnp.where(even, roll(low, -HALF), high))
    return plus, minus


def moments_kernel(
    count, height, counts_ref, box_ref, positions_ref, charges_ref,
    totals_ref, decay_ref, before_ref, table_ref, high_ref, low_ref, phase_ref, weight_ref,
):
    ions = positions_ref.shape[1]
    blocks = ions // BLOCK
    pairs = count // 2
    slab_rank = lax.axis_index("slab")
    mode_rank = lax.axis_index("mode")
    box_x = jnp.full((1, 1), box_ref[0], jnp.float32)
    box_y = jnp.full((1, 1), box_ref[1], jnp.float32)
    live = counts_ref[slab_rank]
    lower_edge = slab_rank.astype(jnp.float32) * height
    scale = (2.0 * two_pi) / (box_x * box_y)

    plus, minus = table_terms(count, height, box_x, box_y)
    for m in range(pairs):
        table_ref[0, :, m * LANES : (m + 1) * LANES] = plus[m]
        table_ref[1, :, m * LANES : (m + 1) * LANES] = minus[m]

    rows = iota((8, BLOCK), 0).astype(jnp.float32)
    upward, downward = [], []
    tile = (PDIM, LANES)
    sign = half_sign(tile)
    group_sign = jnp.where(even_group(tile), 1.0, -1.0)
    found = []
    for b in range(blocks):
        span = slice(b * BLOCK, (b + 1) * BLOCK)
        x = positions_ref[0:1, span]
        y = positions_ref[1:2, span]
        t = (positions_ref[2:3, span] - lower_edge) * (2.0 / height) - 1.0
        slot = mode_rank * ions + b * BLOCK + iota((1, BLOCK), 1)
        weight = jnp.where(slot < live, charges_ref[0:1, span], 0.0)
        weight_ref[0:1, span] = weight * scale

        x8 = 8.0 * x
        y8 = 8.0 * y
        x8 = x8 - jnp.floor(x8)
        y8 = y8 - jnp.floor(y8)
        base_c, base_s = turn((rows + 1.0) * x - 0.5 * y)
        step_c, step_s = turn(rows * x8)
        phase_c, phase_s = [base_c], [base_s]
        for m in range(1, PDIM // 8):
            c, s = step_c[m : m + 1], step_s[m : m + 1]
            phase_c.append(base_c * c - base_s * s)
            phase_s.append(base_s * c + base_c * s)
        phase = jnp.concatenate(phase_c + phase_s, axis=0)
        phase_ref[:, span] = phase
        base_c, base_s = turn((rows + 0.5) * y)
        step_c, step_s = turn(rows * y8)
        side_c, side_s = [base_c], [base_s]
        for m in range(1, HALF // 8):
            c, s = step_c[m : m + 1], step_s[m : m + 1]
            side_c.append(base_c * c - base_s * s)
            side_s.append(base_s * c + base_c * s)
        sides = (jnp.concatenate(side_c, axis=0), jnp.concatenate(side_s, axis=0))

        powers = [jnp.ones_like(t), t]
        for n in range(2, count):
            powers.append(2.0 * t * powers[-1] - powers[-2])
        for m in range(pairs):
            for part in range(2):
                for parity in range(2):
                    at = m * LANES + part * 2 * HALF + parity * HALF
                    high, low = split(powers[2 * m + parity] * sides[part])
                    high_ref[at : at + HALF, span] = high
                    low_ref[at : at + HALF, span] = low

        heavy_high, heavy_low = split(phase * weight)
        both = jnp.concatenate([heavy_high, heavy_low], axis=0)
        across = (((1,), (1,)), ((), ()))
        first = lax.dot_general(both, high_ref[:, span], across, preferred_element_type=jnp.float32)
        second = lax.dot_general(heavy_high, low_ref[:, span], across, preferred_element_type=jnp.float32)
        moments = first[: 2 * PDIM] + first[2 * PDIM :] + second

        sums = [jnp.zeros(tile, jnp.float32) for _ in range(4)]
        for m in range(pairs):
            piece = moments[:, m * LANES : (m + 1) * LANES]
            for kind, values in enumerate((plus[m], minus[m])):
                sums[2 * kind] += values * piece[:PDIM]
                sums[2 * kind + 1] += values * piece[PDIM:]
        added = sums[0] + sign * roll(sums[1], LANES // 2)
        taken = roll(sums[3], LANES // 2) - sign * sums[2]
        found.append([swap_groups(v) + group_sign * v for v in (added, taken)])

    p, q_plus, q_minus = tile_orders()
    even = even_group(tile)
    for kind, order_q in enumerate((q_plus, q_minus)):
        wave_norm = wave(p, order_q, box_x, box_y)[2]
        boost = jnp.exp(wave_norm * height)
        prefix = [jnp.zeros(tile, jnp.float32)]
        for b in range(blocks):
            prefix.append(prefix[-1] + found[b][kind])
        total = prefix[-1]
        for b in range(blocks):
            before_ref[b, kind] = boost * jnp.where(even, prefix[b], total - prefix[b + 1])
        top, bottom = total[: PDIM // 2], total[PDIM // 2 :]
        small = even_group(top.shape)
        totals_ref[kind, 0] = jnp.where(small, top, roll(bottom, HALF))
        totals_ref[kind, 1] = jnp.where(small, roll(top, -HALF), bottom)
        depth = wave_norm * height
        decay_ref[kind] = jnp.where(small, depth[: PDIM // 2], depth[PDIM // 2 :])


def forces_kernel(
    count, box_ref, carry_ref, before_ref, table_ref, high_ref, low_ref, phase_ref, weight_ref,
    forces_ref, coarse_ref, fine_ref,
):
    blocks = before_ref.shape[0]
    pairs = count // 2
    box_x = jnp.full((1, 1), box_ref[0], jnp.float32)
    box_y = jnp.full((1, 1), box_ref[1], jnp.float32)
    tile = (PDIM, LANES)
    sign = half_sign(tile)
    group_sign = jnp.where(even_group(tile), 1.0, -1.0)
    p, q_plus, q_minus = tile_orders()
    base, units = [], []
    small = even_group((PDIM // 2, LANES))
    for kind, order_q in enumerate((q_plus, q_minus)):
        up, down = carry_ref[kind, 0], carry_ref[kind, 1]
        top = jnp.where(small, up, roll(down, HALF))
        bottom = jnp.where(small, roll(up, -HALF), down)
        base.append(jnp.concatenate([top, bottom], axis=0))
        wave_x, wave_y, wave_norm = wave(p, order_q, box_x, box_y)
        units.append((wave_x / wave_norm, wave_y / wave_norm))

    for b in range(blocks):
        span = slice(b * BLOCK, (b + 1) * BLOCK)
        sides = []
        for kind in range(2):
            held = base[kind] + before_ref[b, kind]
            mixed = held + group_sign * swap_groups(held)
            turned = sign * roll(mixed, LANES // 2)
            sides.append((units[kind][0] * turned, units[kind][1] * turned, -swap_groups(mixed)))
        for o in range(3):
            plus, minus = sides[0][o], sides[1][o]
            plus_rows = (plus, -sign * roll(plus, LANES // 2))
            minus_rows = (-sign * minus, roll(minus, LANES // 2))
            for m in range(pairs):
                lanes = slice(m * LANES, (m + 1) * LANES)
                table_plus = table_ref[0, :, lanes]
                table_minus = table_ref[1, :, lanes]
                for part in range(2):
                    at = (2 * o + part) * PDIM
                    high, low = split(table_plus * plus_rows[part] + table_minus * minus_rows[part])
                    coarse_ref[at : at + PDIM, lanes] = high
                    fine_ref[at : at + PDIM, lanes] = low
        field = jnp.dot(coarse_ref[...], high_ref[:, span], preferred_element_type=jnp.float32)
        field += jnp.dot(fine_ref[...], high_ref[:, span], preferred_element_type=jnp.float32)
        field += jnp.dot(coarse_ref[...], low_ref[:, span], preferred_element_type=jnp.float32)
        phase = phase_ref[:, span]
        for o in range(3):
            part = field[o * 2 * PDIM : (o + 1) * 2 * PDIM]
            forces_ref[o : o + 1, span] = jnp.sum(phase * part, axis=0, keepdims=True) * weight_ref[0:1, span]


def shards(positions, charges, counts, box):
    slab_count = lax.axis_size("slab")
    mode_parts = lax.axis_size("mode")
    slab_rank = lax.axis_index("slab")
    mode_rank = lax.axis_index("mode")
    height = slab_span / slab_count
    count = series_terms(height)
    ions = positions.shape[1]
    blocks = ions // BLOCK
    terms = count * 2 * HALF
    scalar = pl.BlockSpec(memory_space=pltpu.SMEM)
    vector = pl.BlockSpec(memory_space=pltpu.VMEM)
    params = pltpu.CompilerParams(vmem_limit_bytes=48 * 1024 * 1024)
    half = PDIM // 2
    totals, decay, before, table, high, low, phase, weight = pl.pallas_call(
        functools.partial(moments_kernel, count, height),
        out_shape=[
            pltpu.VMEM((2, 2, half, LANES), jnp.float32),
            pltpu.VMEM((2, half, LANES), jnp.float32),
            pltpu.VMEM((blocks, 2, PDIM, LANES), jnp.float32),
            pltpu.VMEM((2, PDIM, terms), jnp.float32),
            pltpu.VMEM((terms, ions), jnp.bfloat16),
            pltpu.VMEM((terms, ions), jnp.bfloat16),
            pltpu.VMEM((2 * PDIM, ions), jnp.float32),
            pltpu.VMEM((1, ions), jnp.float32),
        ],
        in_specs=[scalar, scalar, vector, vector],
        out_specs=[vector] * 8,
        compiler_params=params,
        name="moments",
    )(counts, box, positions, charges[None, :])

    gathered = lax.all_gather(totals, "mode", axis=0)
    slab_totals = jnp.sum(gathered, axis=0)
    slab_ids = jnp.arange(slab_count, dtype=jnp.int32)[:, None, None, None]
    sent = jnp.where(slab_ids > slab_rank, slab_totals[None, :, 0], slab_totals[None, :, 1])
    got = lax.all_to_all(sent, "slab", split_axis=0, concat_axis=0, tiled=True)
    gap = jnp.maximum(jnp.abs(slab_ids - slab_rank) - 1, 0).astype(jnp.float32)
    got = got * jnp.exp(-decay[None] * gap)
    boost = jnp.exp(decay)
    mode_ids = jnp.arange(mode_parts, dtype=jnp.int32)[:, None, None, None]
    up = jnp.sum(jnp.where(slab_ids < slab_rank, got, 0.0), axis=0)
    down = jnp.sum(jnp.where(slab_ids > slab_rank, got, 0.0), axis=0)
    up += boost * jnp.sum(jnp.where(mode_ids < mode_rank, gathered[:, :, 0], 0.0), axis=0)
    down += boost * jnp.sum(jnp.where(mode_ids > mode_rank, gathered[:, :, 1], 0.0), axis=0)
    carry = jnp.stack([up, down], axis=1)

    kept = [pltpu.with_memory_space_constraint(v, pltpu.VMEM) for v in (before, table, high, low, phase, weight)]
    return pl.pallas_call(
        functools.partial(forces_kernel, count),
        out_shape=jax.ShapeDtypeStruct((3, ions), jnp.float32),
        in_specs=[scalar] + [vector] * 7,
        out_specs=vector,
        scratch_shapes=[
            pltpu.VMEM((6 * PDIM, terms), jnp.bfloat16),
            pltpu.VMEM((6 * PDIM, terms), jnp.bfloat16),
        ],
        compiler_params=params,
        name="forces",
    )(box, carry, *kept)


def solution(mesh):
    return jax.shard_map(
        shards,
        mesh=mesh,
        in_specs=(P(None, ("slab", "mode")), P(("slab", "mode")), P(), P()),
        out_specs=P(None, ("slab", "mode")),
        check_vma=False,
    )
```

```python
import functools
import math

import jax
import jax.numpy as jnp
import numpy as np
from jax import lax
from jax.experimental import pallas as pl
from jax.experimental.pallas import tpu as pltpu
from jax.sharding import PartitionSpec as P

QDIM = 64
BLOCK = 512
MODES = 4096
PDIM = MODES // QDIM
HALF = QDIM // 2
LANES = 4 * HALF

two_pi = 2.0 * math.pi
slab_span = 0.08
box_low = 0.8

SIN_TERMS = (3.14159264, -5.16771008, 2.55007752, -0.59829129, 0.07765766)
COS_TERMS = (1.0, -4.93480214, 4.05870916, -1.335212, 0.23493731, -0.02439632)


def series_terms(height):
    a = 0.5 * height * two_pi * math.hypot(PDIM, HALF) / box_low
    nodes = np.cos(np.pi * (np.arange(64) + 0.5) / 64)
    order = np.arange(32)[:, None]
    coefficients = np.abs((np.exp(-a * (1.0 + nodes)) * np.cos(order * np.arccos(nodes))).sum(1) / 32.0)
    count = 4
    while coefficients[count:].sum() > 2.0**-24:
        count += 4
    return count


def poly(terms, u):
    value = jnp.full_like(u, terms[-1])
    for term in terms[-2::-1]:
        value = value * u + term
    return value


def turn(angle):
    r = angle - jnp.floor(angle + 0.5)
    u = r * r
    s = r * poly(SIN_TERMS, u)
    c = poly(COS_TERMS, u)
    return 1.0 - 2.0 * s * s, 2.0 * s * c


def split(x):
    high = x.astype(jnp.bfloat16)
    return high, (x - high.astype(jnp.float32)).astype(jnp.bfloat16)


def iota(shape, dim):
    return lax.broadcasted_iota(jnp.int32, shape, dim)


def roll(x, shift):
    return pltpu.roll(x, shift % LANES, x.ndim - 1)


def even_group(shape):
    return (iota(shape, 1) // HALF) % 2 == 0


def swap_groups(x):
    return jnp.where(even_group(x.shape), roll(x, -HALF), roll(x, HALF))


def half_sign(shape):
    return jnp.where(iota(shape, 1) < LANES // 2, -1.0, 1.0)


def wave(order_p, order_q, box_x, box_y):
    wave_x = two_pi * order_p / box_x
    wave_y = two_pi * order_q / box_y
    return wave_x, wave_y, jnp.sqrt(wave_x * wave_x + wave_y * wave_y)


def tile_orders():
    shape = (PDIM, LANES)
    p = (iota(shape, 0) + 1).astype(jnp.float32)
    j = iota(shape, 1) % HALF
    return p, j.astype(jnp.float32), (-1 - j).astype(jnp.float32)


def table_terms(count, height, box_x, box_y):
    p, q_plus, q_minus = tile_orders()
    even = even_group(p.shape)
    a = (0.5 * height) * wave(p, jnp.where(even, q_plus, q_minus), box_x, box_y)[2]
    ratio = jnp.zeros_like(a)
    ratios = {}
    for n in range(count + 6, 0, -1):
        ratio = a / (2.0 * n + a * ratio)
        ratios[n] = ratio
    products = [jnp.ones_like(a)]
    total = jnp.ones_like(a)
    for n in range(1, count + 7):
        products.append(products[-1] * ratios[n])
        total = total + 2.0 * products[n]
    first = 1.0 / total
    terms = [first] + [(2.0 * first) * products[n] for n in range(1, count)]
    plus, minus = [], []
    for m in range(count // 2):
        low, high = terms[2 * m], terms[2 * m + 1]
        plus.append(jnp.where(even, low, roll(high, HALF)))
        minus.append(jnp.where(even, roll(low, -HALF), high))
    return plus, minus


def moments_kernel(
    count, height, counts_ref, box_ref, positions_ref, charges_ref,
    totals_ref, decay_ref, before_ref, table_ref, weight_ref, high_out, low_out, phase_out,
    high_ref, low_ref, phase_ref, sems,
):
    ions = positions_ref.shape[1]
    blocks = ions // BLOCK
    pairs = count // 2
    slab_rank = lax.axis_index("slab")
    mode_rank = lax.axis_index("mode")
    box_x = jnp.full((1, 1), box_ref[0], jnp.float32)
    box_y = jnp.full((1, 1), box_ref[1], jnp.float32)
    live = counts_ref[slab_rank]
    lower_edge = slab_rank.astype(jnp.float32) * height
    scale = (2.0 * two_pi) / (box_x * box_y)

    plus, minus = table_terms(count, height, box_x, box_y)
    for m in range(pairs):
        table_ref[0, :, m * LANES : (m + 1) * LANES] = plus[m]
        table_ref[1, :, m * LANES : (m + 1) * LANES] = minus[m]

    rows = iota((8, BLOCK), 0).astype(jnp.float32)
    upward, downward = [], []
    tile = (PDIM, LANES)
    sign = half_sign(tile)
    group_sign = jnp.where(even_group(tile), 1.0, -1.0)
    found, copies = [], []
    for b in range(blocks):
        span = slice(b * BLOCK, (b + 1) * BLOCK)
        x = positions_ref[0:1, span]
        y = positions_ref[1:2, span]
        t = (positions_ref[2:3, span] - lower_edge) * (2.0 / height) - 1.0
        slot = mode_rank * ions + b * BLOCK + iota((1, BLOCK), 1)
        weight = jnp.where(slot < live, charges_ref[0:1, span], 0.0)
        weight_ref[0:1, span] = weight * scale

        x8 = 8.0 * x
        y8 = 8.0 * y
        x8 = x8 - jnp.floor(x8)
        y8 = y8 - jnp.floor(y8)
        base_c, base_s = turn((rows + 1.0) * x - 0.5 * y)
        step_c, step_s = turn(rows * x8)
        phase_c, phase_s = [base_c], [base_s]
        for m in range(1, PDIM // 8):
            c, s = step_c[m : m + 1], step_s[m : m + 1]
            phase_c.append(base_c * c - base_s * s)
            phase_s.append(base_s * c + base_c * s)
        phase = jnp.concatenate(phase_c + phase_s, axis=0)
        phase_ref[b] = phase
        base_c, base_s = turn((rows + 0.5) * y)
        step_c, step_s = turn(rows * y8)
        side_c, side_s = [base_c], [base_s]
        for m in range(1, HALF // 8):
            c, s = step_c[m : m + 1], step_s[m : m + 1]
            side_c.append(base_c * c - base_s * s)
            side_s.append(base_s * c + base_c * s)
        sides = (jnp.concatenate(side_c, axis=0), jnp.concatenate(side_s, axis=0))

        powers = [jnp.ones_like(t), t]
        for n in range(2, count):
            powers.append(2.0 * t * powers[-1] - powers[-2])
        for m in range(pairs):
            for part in range(2):
                for parity in range(2):
                    at = m * LANES + part * 2 * HALF + parity * HALF
                    high, low = split(powers[2 * m + parity] * sides[part])
                    high_ref[b, at : at + HALF] = high
                    low_ref[b, at : at + HALF] = low
        for i, (held, out) in enumerate(((high_ref, high_out), (low_ref, low_out), (phase_ref, phase_out))):
            copies.append(pltpu.make_async_copy(held.at[b], out.at[b], sems.at[i, b]))
            copies[-1].start()

        heavy_high, heavy_low = split(phase * weight)
        both = jnp.concatenate([heavy_high, heavy_low], axis=0)
        across = (((1,), (1,)), ((), ()))
        first = lax.dot_general(both, high_ref[b], across, preferred_element_type=jnp.float32)
        second = lax.dot_general(heavy_high, low_ref[b], across, preferred_element_type=jnp.float32)
        moments = first[: 2 * PDIM] + first[2 * PDIM :] + second

        sums = [jnp.zeros(tile, jnp.float32) for _ in range(4)]
        for m in range(pairs):
            piece = moments[:, m * LANES : (m + 1) * LANES]
            for kind, values in enumerate((plus[m], minus[m])):
                sums[2 * kind] += values * piece[:PDIM]
                sums[2 * kind + 1] += values * piece[PDIM:]
        added = sums[0] + sign * roll(sums[1], LANES // 2)
        taken = roll(sums[3], LANES // 2) - sign * sums[2]
        found.append([swap_groups(v) + group_sign * v for v in (added, taken)])

    p, q_plus, q_minus = tile_orders()
    even = even_group(tile)
    for kind, order_q in enumerate((q_plus, q_minus)):
        wave_norm = wave(p, order_q, box_x, box_y)[2]
        boost = jnp.exp(wave_norm * height)
        prefix = [jnp.zeros(tile, jnp.float32)]
        for b in range(blocks):
            prefix.append(prefix[-1] + found[b][kind])
        total = prefix[-1]
        for b in range(blocks):
            before_ref[b, kind] = boost * jnp.where(even, prefix[b], total - prefix[b + 1])
        top, bottom = total[: PDIM // 2], total[PDIM // 2 :]
        small = even_group(top.shape)
        totals_ref[kind, 0] = jnp.where(small, top, roll(bottom, HALF))
        totals_ref[kind, 1] = jnp.where(small, roll(top, -HALF), bottom)
        depth = wave_norm * height
        decay_ref[kind] = jnp.where(small, depth[: PDIM // 2], depth[PDIM // 2 :])
    for copy in copies:
        copy.wait()


def forces_kernel(
    count, box_ref, carry_ref, before_ref, table_ref, weight_ref, high_in, low_in, phase_in,
    forces_ref, coarse_ref, fine_ref, high_ref, low_ref, phase_ref, sems,
):
    blocks = before_ref.shape[0]
    copies = []
    for b in range(blocks):
        for i, (source, held) in enumerate(((high_in, high_ref), (low_in, low_ref), (phase_in, phase_ref))):
            copies.append(pltpu.make_async_copy(source.at[b], held.at[b], sems.at[i, b]))
            copies[-1].start()
    pairs = count // 2
    box_x = jnp.full((1, 1), box_ref[0], jnp.float32)
    box_y = jnp.full((1, 1), box_ref[1], jnp.float32)
    tile = (PDIM, LANES)
    sign = half_sign(tile)
    group_sign = jnp.where(even_group(tile), 1.0, -1.0)
    p, q_plus, q_minus = tile_orders()
    base, units = [], []
    small = even_group((PDIM // 2, LANES))
    for kind, order_q in enumerate((q_plus, q_minus)):
        up, down = carry_ref[kind, 0], carry_ref[kind, 1]
        top = jnp.where(small, up, roll(down, HALF))
        bottom = jnp.where(small, roll(up, -HALF), down)
        base.append(jnp.concatenate([top, bottom], axis=0))
        wave_x, wave_y, wave_norm = wave(p, order_q, box_x, box_y)
        units.append((wave_x / wave_norm, wave_y / wave_norm))

    for b in range(blocks):
        span = slice(b * BLOCK, (b + 1) * BLOCK)
        sides = []
        for kind in range(2):
            held = base[kind] + before_ref[b, kind]
            mixed = held + group_sign * swap_groups(held)
            turned = sign * roll(mixed, LANES // 2)
            sides.append((units[kind][0] * turned, units[kind][1] * turned, -swap_groups(mixed)))
        for o in range(3):
            plus, minus = sides[0][o], sides[1][o]
            plus_rows = (plus, -sign * roll(plus, LANES // 2))
            minus_rows = (-sign * minus, roll(minus, LANES // 2))
            for m in range(pairs):
                lanes = slice(m * LANES, (m + 1) * LANES)
                table_plus = table_ref[0, :, lanes]
                table_minus = table_ref[1, :, lanes]
                for part in range(2):
                    at = (2 * o + part) * PDIM
                    high, low = split(table_plus * plus_rows[part] + table_minus * minus_rows[part])
                    coarse_ref[at : at + PDIM, lanes] = high
                    fine_ref[at : at + PDIM, lanes] = low
        for copy in copies[3 * b : 3 * b + 3]:
            copy.wait()
        field = jnp.dot(coarse_ref[...], high_ref[b], preferred_element_type=jnp.float32)
        field += jnp.dot(fine_ref[...], high_ref[b], preferred_element_type=jnp.float32)
        field += jnp.dot(coarse_ref[...], low_ref[b], preferred_element_type=jnp.float32)
        phase = phase_ref[b]
        for o in range(3):
            part = field[o * 2 * PDIM : (o + 1) * 2 * PDIM]
            forces_ref[o : o + 1, span] = jnp.sum(phase * part, axis=0, keepdims=True) * weight_ref[0:1, span]


def exchange(totals, decay, parts, axis):
    rank = lax.axis_index(axis)
    part = jnp.arange(2, dtype=jnp.int32)[None, :, None, None]
    outside = jnp.zeros_like(totals)
    stride = 1
    while stride < parts:
        other = lax.ppermute(totals, axis, [(i, i ^ stride) for i in range(parts)])
        upper = (rank // stride) % 2
        ahead = part != upper
        below = rank % stride
        steps = jnp.where(part == 0, below, stride - 1 - below)
        if decay is None:
            outside = outside + jnp.where(ahead, other, 0.0)
            totals = totals + other
        else:
            outside = outside + jnp.where(ahead, other * jnp.exp(-decay * steps.astype(jnp.float32)), 0.0)
            fade = jnp.exp(-decay * float(stride))
            totals = jnp.where(ahead, totals + fade * other, other + fade * totals)
        stride *= 2
    return outside, totals


def shards(positions, charges, counts, box):
    slab_count = lax.axis_size("slab")
    mode_parts = lax.axis_size("mode")
    height = slab_span / slab_count
    count = series_terms(height)
    ions = positions.shape[1]
    blocks = ions // BLOCK
    terms = count * 2 * HALF
    half = PDIM // 2
    scalar = pl.BlockSpec(memory_space=pltpu.SMEM)
    vector = pl.BlockSpec(memory_space=pltpu.VMEM)
    apart = pl.BlockSpec(memory_space=pltpu.HBM)
    params = pltpu.CompilerParams(vmem_limit_bytes=24 * 1024 * 1024)
    kept = [((blocks, terms, BLOCK), jnp.bfloat16)] * 2 + [((blocks, 2 * PDIM, BLOCK), jnp.float32)]
    held = [pltpu.VMEM(*v) for v in kept] + [pltpu.SemaphoreType.DMA((3, blocks))]
    counts, box, positions, charges = [
        pltpu.with_memory_space_constraint(v, pltpu.HBM) for v in (counts, box, positions, charges[None, :])
    ]
    totals, decay, *small, high, low, phase = pl.pallas_call(
        functools.partial(moments_kernel, count, height),
        out_shape=[
            pltpu.VMEM((2, 2, half, LANES), jnp.float32),
            pltpu.VMEM((2, half, LANES), jnp.float32),
            pltpu.VMEM((blocks, 2, PDIM, LANES), jnp.float32),
            pltpu.VMEM((2, PDIM, terms), jnp.float32),
            pltpu.VMEM((1, ions), jnp.float32),
        ] + [pltpu.HBM(*v) for v in kept],
        in_specs=[scalar, scalar, vector, vector],
        out_specs=[vector] * 5 + [apart] * 3,
        scratch_shapes=held,
        compiler_params=params,
        name="moments",
    )(counts, box, positions, charges)

    inside, slab_totals = exchange(totals, None, mode_parts, "mode")
    depth = decay[:, None]
    carry, _ = exchange(slab_totals, depth, slab_count, "slab")
    carry = carry + jnp.exp(depth) * inside

    carry, *small = [pltpu.with_memory_space_constraint(v, pltpu.VMEM) for v in (carry, *small)]
    high, low, phase = [pltpu.with_memory_space_constraint(v, pltpu.HBM) for v in (high, low, phase)]
    return pl.pallas_call(
        functools.partial(forces_kernel, count),
        out_shape=jax.ShapeDtypeStruct((3, ions), jnp.float32),
        in_specs=[scalar] + [vector] * 4 + [apart] * 3,
        out_specs=vector,
        scratch_shapes=[
            pltpu.VMEM((6 * PDIM, terms), jnp.bfloat16),
            pltpu.VMEM((6 * PDIM, terms), jnp.bfloat16),
        ] + held,
        compiler_params=params,
        name="forces",
    )(box, carry, *small, high, low, phase)


def solution(mesh):
    return jax.shard_map(
        shards,
        mesh=mesh,
        in_specs=(P(None, ("slab", "mode")), P(("slab", "mode")), P(), P()),
        out_specs=P(None, ("slab", "mode")),
        check_vma=False,
    )
```

```python
import functools
import math

import jax
import jax.numpy as jnp
import numpy as np
from jax import lax
from jax.experimental import pallas as pl
from jax.experimental.pallas import tpu as pltpu
from jax.sharding import PartitionSpec as P

QDIM = 64
BLOCK = 512
MODES = 4096
PDIM = MODES // QDIM
HALF = QDIM // 2
LANES = 4 * HALF

two_pi = 2.0 * math.pi
slab_span = 0.08
box_low = 0.8

SIN_TERMS = (3.14159264, -5.16771008, 2.55007752, -0.59829129, 0.07765766)
COS_TERMS = (1.0, -4.93480214, 4.05870916, -1.335212, 0.23493731, -0.02439632)


def series_terms(height):
    a = 0.5 * height * two_pi * math.hypot(PDIM, HALF) / box_low
    nodes = np.cos(np.pi * (np.arange(64) + 0.5) / 64)
    order = np.arange(32)[:, None]
    coefficients = np.abs((np.exp(-a * (1.0 + nodes)) * np.cos(order * np.arccos(nodes))).sum(1) / 32.0)
    count = 4
    while coefficients[count:].sum() > 2.0**-24:
        count += 4
    return count


def poly(terms, u):
    value = jnp.full_like(u, terms[-1])
    for term in terms[-2::-1]:
        value = value * u + term
    return value


def turn(angle):
    r = angle - jnp.floor(angle + 0.5)
    u = r * r
    s = r * poly(SIN_TERMS, u)
    c = poly(COS_TERMS, u)
    return 1.0 - 2.0 * s * s, 2.0 * s * c


def split(x):
    high = x.astype(jnp.bfloat16)
    return high, (x - high.astype(jnp.float32)).astype(jnp.bfloat16)


def iota(shape, dim):
    return lax.broadcasted_iota(jnp.int32, shape, dim)


def roll(x, shift):
    return pltpu.roll(x, shift % LANES, x.ndim - 1)


def even_group(shape):
    return (iota(shape, 1) // HALF) % 2 == 0


def swap_groups(x):
    return jnp.where(even_group(x.shape), roll(x, -HALF), roll(x, HALF))


def half_sign(shape):
    return jnp.where(iota(shape, 1) < LANES // 2, -1.0, 1.0)


def wave(order_p, order_q, box_x, box_y):
    wave_x = two_pi * order_p / box_x
    wave_y = two_pi * order_q / box_y
    return wave_x, wave_y, jnp.sqrt(wave_x * wave_x + wave_y * wave_y)


def tile_orders():
    shape = (PDIM, LANES)
    p = (iota(shape, 0) + 1).astype(jnp.float32)
    j = iota(shape, 1) % HALF
    return p, j.astype(jnp.float32), (-1 - j).astype(jnp.float32)


def table_terms(count, height, box_x, box_y):
    p, q_plus, q_minus = tile_orders()
    even = even_group(p.shape)
    a = (0.5 * height) * wave(p, jnp.where(even, q_plus, q_minus), box_x, box_y)[2]
    ratio = jnp.zeros_like(a)
    ratios = {}
    for n in range(count + 6, 0, -1):
        ratio = a / (2.0 * n + a * ratio)
        ratios[n] = ratio
    products = [jnp.ones_like(a)]
    total = jnp.ones_like(a)
    for n in range(1, count + 7):
        products.append(products[-1] * ratios[n])
        total = total + 2.0 * products[n]
    first = 1.0 / total
    terms = [first] + [(2.0 * first) * products[n] for n in range(1, count)]
    plus, minus = [], []
    for m in range(count // 2):
        low, high = terms[2 * m], terms[2 * m + 1]
        plus.append(jnp.where(even, low, roll(high, HALF)))
        minus.append(jnp.where(even, roll(low, -HALF), high))
    return plus, minus


def spread(count, powers, sides, high_ref, low_ref):
    for m in range(count // 2):
        for part in range(2):
            for parity in range(2):
                at = m * LANES + part * 2 * HALF + parity * HALF
                n = 2 * m + parity
                high, low = split(powers[n : n + 1] * sides[part * HALF : (part + 1) * HALF])
                high_ref[at : at + HALF] = high
                low_ref[at : at + HALF] = low


def moments_kernel(
    count, height, counts_ref, box_ref, positions_ref, charges_ref,
    totals_ref, decay_ref, before_ref, table_ref, weight_ref, phase_ref, sides_ref, powers_ref,
    high_ref, low_ref,
):
    ions = positions_ref.shape[1]
    blocks = ions // BLOCK
    pairs = count // 2
    slab_rank = lax.axis_index("slab")
    mode_rank = lax.axis_index("mode")
    box_x = jnp.full((1, 1), box_ref[0], jnp.float32)
    box_y = jnp.full((1, 1), box_ref[1], jnp.float32)
    live = counts_ref[slab_rank]
    lower_edge = slab_rank.astype(jnp.float32) * height
    scale = (2.0 * two_pi) / (box_x * box_y)

    plus, minus = table_terms(count, height, box_x, box_y)
    for m in range(pairs):
        table_ref[0, :, m * LANES : (m + 1) * LANES] = plus[m]
        table_ref[1, :, m * LANES : (m + 1) * LANES] = minus[m]

    rows = iota((8, BLOCK), 0).astype(jnp.float32)
    upward, downward = [], []
    tile = (PDIM, LANES)
    sign = half_sign(tile)
    group_sign = jnp.where(even_group(tile), 1.0, -1.0)
    found = []
    for b in range(blocks):
        span = slice(b * BLOCK, (b + 1) * BLOCK)
        x = positions_ref[0:1, span]
        y = positions_ref[1:2, span]
        t = (positions_ref[2:3, span] - lower_edge) * (2.0 / height) - 1.0
        slot = mode_rank * ions + b * BLOCK + iota((1, BLOCK), 1)
        weight = jnp.where(slot < live, charges_ref[0:1, span], 0.0)
        weight_ref[0:1, span] = weight * scale

        x8 = 8.0 * x
        y8 = 8.0 * y
        x8 = x8 - jnp.floor(x8)
        y8 = y8 - jnp.floor(y8)
        base_c, base_s = turn((rows + 1.0) * x - 0.5 * y)
        step_c, step_s = turn(rows * x8)
        phase_c, phase_s = [base_c], [base_s]
        for m in range(1, PDIM // 8):
            c, s = step_c[m : m + 1], step_s[m : m + 1]
            phase_c.append(base_c * c - base_s * s)
            phase_s.append(base_s * c + base_c * s)
        phase = jnp.concatenate(phase_c + phase_s, axis=0)
        phase_ref[b] = phase
        base_c, base_s = turn((rows + 0.5) * y)
        step_c, step_s = turn(rows * y8)
        side_c, side_s = [base_c], [base_s]
        for m in range(1, HALF // 8):
            c, s = step_c[m : m + 1], step_s[m : m + 1]
            side_c.append(base_c * c - base_s * s)
            side_s.append(base_s * c + base_c * s)
        sides = jnp.concatenate(side_c + side_s, axis=0)
        sides_ref[b] = sides

        powers = [jnp.ones_like(t), t]
        for n in range(2, count):
            powers.append(2.0 * t * powers[-1] - powers[-2])
        powers = jnp.concatenate(powers, axis=0)
        powers_ref[b] = powers
        spread(count, powers, sides, high_ref.at[b], low_ref.at[b])

        heavy_high, heavy_low = split(phase * weight)
        both = jnp.concatenate([heavy_high, heavy_low], axis=0)
        across = (((1,), (1,)), ((), ()))
        first = lax.dot_general(both, high_ref[b], across, preferred_element_type=jnp.float32)
        second = lax.dot_general(heavy_high, low_ref[b], across, preferred_element_type=jnp.float32)
        moments = first[: 2 * PDIM] + first[2 * PDIM :] + second

        sums = [jnp.zeros(tile, jnp.float32) for _ in range(4)]
        for m in range(pairs):
            piece = moments[:, m * LANES : (m + 1) * LANES]
            for kind, values in enumerate((plus[m], minus[m])):
                sums[2 * kind] += values * piece[:PDIM]
                sums[2 * kind + 1] += values * piece[PDIM:]
        added = sums[0] + sign * roll(sums[1], LANES // 2)
        taken = roll(sums[3], LANES // 2) - sign * sums[2]
        found.append([swap_groups(v) + group_sign * v for v in (added, taken)])

    p, q_plus, q_minus = tile_orders()
    even = even_group(tile)
    for kind, order_q in enumerate((q_plus, q_minus)):
        wave_norm = wave(p, order_q, box_x, box_y)[2]
        boost = jnp.exp(wave_norm * height)
        prefix = [jnp.zeros(tile, jnp.float32)]
        for b in range(blocks):
            prefix.append(prefix[-1] + found[b][kind])
        total = prefix[-1]
        for b in range(blocks):
            before_ref[b, kind] = boost * jnp.where(even, prefix[b], total - prefix[b + 1])
        top, bottom = total[: PDIM // 2], total[PDIM // 2 :]
        small = even_group(top.shape)
        totals_ref[kind, 0] = jnp.where(small, top, roll(bottom, HALF))
        totals_ref[kind, 1] = jnp.where(small, roll(top, -HALF), bottom)
        depth = wave_norm * height
        decay_ref[kind] = jnp.where(small, depth[: PDIM // 2], depth[PDIM // 2 :])


def forces_kernel(
    count, box_ref, carry_ref, before_ref, table_ref, weight_ref, phase_ref, sides_ref, powers_ref,
    forces_ref, coarse_ref, fine_ref, high_ref, low_ref,
):
    blocks = before_ref.shape[0]
    pairs = count // 2
    box_x = jnp.full((1, 1), box_ref[0], jnp.float32)
    box_y = jnp.full((1, 1), box_ref[1], jnp.float32)
    tile = (PDIM, LANES)
    sign = half_sign(tile)
    group_sign = jnp.where(even_group(tile), 1.0, -1.0)
    p, q_plus, q_minus = tile_orders()
    base, units = [], []
    small = even_group((PDIM // 2, LANES))
    for kind, order_q in enumerate((q_plus, q_minus)):
        up, down = carry_ref[kind, 0], carry_ref[kind, 1]
        top = jnp.where(small, up, roll(down, HALF))
        bottom = jnp.where(small, roll(up, -HALF), down)
        base.append(jnp.concatenate([top, bottom], axis=0))
        wave_x, wave_y, wave_norm = wave(p, order_q, box_x, box_y)
        units.append((wave_x / wave_norm, wave_y / wave_norm))

    for b in range(blocks):
        span = slice(b * BLOCK, (b + 1) * BLOCK)
        sides = []
        for kind in range(2):
            held = base[kind] + before_ref[b, kind]
            mixed = held + group_sign * swap_groups(held)
            turned = sign * roll(mixed, LANES // 2)
            sides.append((units[kind][0] * turned, units[kind][1] * turned, -swap_groups(mixed)))
        for o in range(3):
            plus, minus = sides[0][o], sides[1][o]
            plus_rows = (plus, -sign * roll(plus, LANES // 2))
            minus_rows = (-sign * minus, roll(minus, LANES // 2))
            for m in range(pairs):
                lanes = slice(m * LANES, (m + 1) * LANES)
                table_plus = table_ref[0, :, lanes]
                table_minus = table_ref[1, :, lanes]
                for part in range(2):
                    at = (2 * o + part) * PDIM
                    high, low = split(table_plus * plus_rows[part] + table_minus * minus_rows[part])
                    coarse_ref[at : at + PDIM, lanes] = high
                    fine_ref[at : at + PDIM, lanes] = low
        spread(count, powers_ref[b], sides_ref[b], high_ref.at[b], low_ref.at[b])
        field = jnp.dot(coarse_ref[...], high_ref[b], preferred_element_type=jnp.float32)
        field += jnp.dot(fine_ref[...], high_ref[b], preferred_element_type=jnp.float32)
        field += jnp.dot(coarse_ref[...], low_ref[b], preferred_element_type=jnp.float32)
        phase = phase_ref[b]
        for o in range(3):
            part = field[o * 2 * PDIM : (o + 1) * 2 * PDIM]
            forces_ref[o : o + 1, span] = jnp.sum(phase * part, axis=0, keepdims=True) * weight_ref[0:1, span]


def exchange(totals, decay, parts, axis):
    rank = lax.axis_index(axis)
    part = jnp.arange(2, dtype=jnp.int32)[None, :, None, None]
    outside = jnp.zeros_like(totals)
    stride = 1
    while stride < parts:
        upper = (rank // stride) % 2
        ahead = part != upper
        below = rank % stride
        steps = jnp.where(part == 0, below, stride - 1 - below)
        pairs = [(i, i ^ stride) for i in range(parts)]
        if decay is not None and 2 * stride == parts:
            other = lax.ppermute(jnp.where(upper == 0, totals[:, 0], totals[:, 1]), axis, pairs)[:, None]
        else:
            other = lax.ppermute(totals, axis, pairs)
        if decay is None:
            outside = outside + jnp.where(ahead, other, 0.0)
            totals = totals + other
        else:
            outside = outside + jnp.where(ahead, other * jnp.exp(-decay * steps.astype(jnp.float32)), 0.0)
            fade = jnp.exp(-decay * float(stride))
            totals = jnp.where(ahead, totals + fade * other, other + fade * totals)
        stride *= 2
    return outside, totals


def shards(positions, charges, counts, box):
    slab_count = lax.axis_size("slab")
    mode_parts = lax.axis_size("mode")
    height = slab_span / slab_count
    count = series_terms(height)
    ions = positions.shape[1]
    blocks = ions // BLOCK
    terms = count * 2 * HALF
    half = PDIM // 2
    scalar = pl.BlockSpec(memory_space=pltpu.SMEM)
    vector = pl.BlockSpec(memory_space=pltpu.VMEM)
    params = pltpu.CompilerParams(vmem_limit_bytes=24 * 1024 * 1024)
    work = [pltpu.VMEM((blocks, terms, BLOCK), jnp.bfloat16)] * 2
    counts, box, positions, charges = [
        pltpu.with_memory_space_constraint(v, pltpu.HBM) for v in (counts, box, positions, charges[None, :])
    ]
    totals, decay, *kept = pl.pallas_call(
        functools.partial(moments_kernel, count, height),
        out_shape=[
            pltpu.VMEM((2, 2, half, LANES), jnp.float32),
            pltpu.VMEM((2, half, LANES), jnp.float32),
            pltpu.VMEM((blocks, 2, PDIM, LANES), jnp.float32),
            pltpu.VMEM((2, PDIM, terms), jnp.float32),
            pltpu.VMEM((1, ions), jnp.float32),
            pltpu.VMEM((blocks, 2 * PDIM, BLOCK), jnp.float32),
            pltpu.VMEM((blocks, 2 * HALF, BLOCK), jnp.float32),
            pltpu.VMEM((blocks, count, BLOCK), jnp.float32),
        ],
        in_specs=[scalar, scalar, vector, vector],
        out_specs=[vector] * 8,
        scratch_shapes=work,
        compiler_params=params,
        name="moments",
    )(counts, box, positions, charges)

    inside, slab_totals = exchange(totals, None, mode_parts, "mode")
    depth = decay[:, None]
    carry, _ = exchange(slab_totals, depth, slab_count, "slab")
    carry = carry + jnp.exp(depth) * inside

    carry, *kept = [pltpu.with_memory_space_constraint(v, pltpu.VMEM) for v in (carry, *kept)]
    return pl.pallas_call(
        functools.partial(forces_kernel, count),
        out_shape=jax.ShapeDtypeStruct((3, ions), jnp.float32),
        in_specs=[scalar] + [vector] * 7,
        out_specs=vector,
        scratch_shapes=[
            pltpu.VMEM((6 * PDIM, terms), jnp.bfloat16),
            pltpu.VMEM((6 * PDIM, terms), jnp.bfloat16),
        ] + work,
        compiler_params=params,
        name="forces",
    )(box, carry, *kept)


def solution(mesh):
    return jax.shard_map(
        shards,
        mesh=mesh,
        in_specs=(P(None, ("slab", "mode")), P(("slab", "mode")), P(), P()),
        out_specs=P(None, ("slab", "mode")),
        check_vma=False,
    )
```

```python
import functools
import math

import jax
import jax.numpy as jnp
import numpy as np
from jax import lax
from jax.experimental import pallas as pl
from jax.experimental.pallas import tpu as pltpu
from jax.sharding import PartitionSpec as P

QDIM = 64
BLOCK = 512
MODES = 4096
PDIM = MODES // QDIM
HALF = QDIM // 2
LANES = 4 * HALF

two_pi = 2.0 * math.pi
slab_span = 0.08
box_low = 0.8

SIN_TERMS = (3.14159264, -5.16771008, 2.55007752, -0.59829129, 0.07765766)
COS_TERMS = (1.0, -4.93480214, 4.05870916, -1.335212, 0.23493731, -0.02439632)


def series_terms(height):
    a = 0.5 * height * two_pi * math.hypot(PDIM, HALF) / box_low
    nodes = np.cos(np.pi * (np.arange(64) + 0.5) / 64)
    order = np.arange(32)[:, None]
    coefficients = np.abs((np.exp(-a * (1.0 + nodes)) * np.cos(order * np.arccos(nodes))).sum(1) / 32.0)
    count = 4
    while coefficients[count:].sum() > 2.0**-24:
        count += 4
    return count


def poly(terms, u):
    value = jnp.full_like(u, terms[-1])
    for term in terms[-2::-1]:
        value = value * u + term
    return value


def turn(angle):
    r = angle - jnp.floor(angle + 0.5)
    u = r * r
    s = r * poly(SIN_TERMS, u)
    c = poly(COS_TERMS, u)
    return 1.0 - 2.0 * s * s, 2.0 * s * c


def split(x):
    high = x.astype(jnp.bfloat16)
    return high, (x - high.astype(jnp.float32)).astype(jnp.bfloat16)


def iota(shape, dim):
    return lax.broadcasted_iota(jnp.int32, shape, dim)


def roll(x, shift):
    return pltpu.roll(x, shift % LANES, x.ndim - 1)


def even_group(shape):
    return (iota(shape, 1) // HALF) % 2 == 0


def swap_groups(x):
    return jnp.where(even_group(x.shape), roll(x, -HALF), roll(x, HALF))


def half_sign(shape):
    return jnp.where(iota(shape, 1) < LANES // 2, -1.0, 1.0)


def wave(order_p, order_q, box_x, box_y):
    wave_x = two_pi * order_p / box_x
    wave_y = two_pi * order_q / box_y
    return wave_x, wave_y, jnp.sqrt(wave_x * wave_x + wave_y * wave_y)


def tile_orders():
    shape = (PDIM, LANES)
    p = (iota(shape, 0) + 1).astype(jnp.float32)
    j = iota(shape, 1) % HALF
    return p, j.astype(jnp.float32), (-1 - j).astype(jnp.float32)


def table_terms(count, height, box_x, box_y):
    p, q_plus, q_minus = tile_orders()
    even = even_group(p.shape)
    a = (0.5 * height) * wave(p, jnp.where(even, q_plus, q_minus), box_x, box_y)[2]
    square = 0.25 * a * a
    last = count + 8
    scaled = {last + 1: jnp.ones_like(a), last: jnp.ones_like(a)}
    for n in range(last, 0, -1):
        scaled[n - 1] = scaled[n] + square * (scaled[n + 1] * (1.0 / (n * (n + 1))))
    power, total = jnp.ones_like(a), scaled[0]
    parts = [scaled[0]]
    for n in range(1, last + 1):
        power = power * (a * (0.5 / n))
        parts.append(2.0 * (power * scaled[n]))
        total = total + parts[n]
    first = 1.0 / total
    terms = [first * part for part in parts[:count]]
    plus, minus = [], []
    for m in range(count // 2):
        low, high = terms[2 * m], terms[2 * m + 1]
        plus.append(jnp.where(even, low, roll(high, HALF)))
        minus.append(jnp.where(even, roll(low, -HALF), high))
    return plus, minus


def spread(count, powers, sides, high_ref, low_ref):
    for m in range(count // 2):
        for part in range(2):
            for parity in range(2):
                at = m * LANES + part * 2 * HALF + parity * HALF
                n = 2 * m + parity
                high, low = split(powers[n : n + 1] * sides[part * HALF : (part + 1) * HALF])
                high_ref[at : at + HALF] = high
                low_ref[at : at + HALF] = low


def moments_kernel(
    count, height, counts_ref, box_ref, positions_ref, charges_ref,
    totals_ref, decay_ref, unit_ref, before_ref, table_ref, weight_ref, phase_ref, sides_ref, powers_ref,
    high_ref, low_ref,
):
    ions = positions_ref.shape[1]
    blocks = ions // BLOCK
    pairs = count // 2
    slab_rank = lax.axis_index("slab")
    mode_rank = lax.axis_index("mode")
    box_x = jnp.full((1, 1), box_ref[0], jnp.float32)
    box_y = jnp.full((1, 1), box_ref[1], jnp.float32)
    live = counts_ref[slab_rank]
    lower_edge = slab_rank.astype(jnp.float32) * height
    scale = (2.0 * two_pi) / (box_x * box_y)

    plus, minus = table_terms(count, height, box_x, box_y)
    for m in range(pairs):
        table_ref[0, :, m * LANES : (m + 1) * LANES] = plus[m]
        table_ref[1, :, m * LANES : (m + 1) * LANES] = minus[m]

    rows = iota((8, BLOCK), 0).astype(jnp.float32)
    upward, downward = [], []
    tile = (PDIM, LANES)
    sign = half_sign(tile)
    group_sign = jnp.where(even_group(tile), 1.0, -1.0)
    found = []
    for b in range(blocks):
        span = slice(b * BLOCK, (b + 1) * BLOCK)
        x = positions_ref[0:1, span]
        y = positions_ref[1:2, span]
        t = (positions_ref[2:3, span] - lower_edge) * (2.0 / height) - 1.0
        slot = mode_rank * ions + b * BLOCK + iota((1, BLOCK), 1)
        weight = jnp.where(slot < live, charges_ref[0:1, span], 0.0)
        weight_ref[0:1, span] = weight * scale

        x8 = 8.0 * x
        y8 = 8.0 * y
        x8 = x8 - jnp.floor(x8)
        y8 = y8 - jnp.floor(y8)
        base_c, base_s = turn((rows + 1.0) * x - 0.5 * y)
        step_c, step_s = turn(rows * x8)
        phase_c, phase_s = [base_c], [base_s]
        for m in range(1, PDIM // 8):
            c, s = step_c[m : m + 1], step_s[m : m + 1]
            phase_c.append(base_c * c - base_s * s)
            phase_s.append(base_s * c + base_c * s)
        phase = jnp.concatenate(phase_c + phase_s, axis=0)
        phase_ref[b] = phase
        base_c, base_s = turn((rows + 0.5) * y)
        step_c, step_s = turn(rows * y8)
        side_c, side_s = [base_c], [base_s]
        for m in range(1, HALF // 8):
            c, s = step_c[m : m + 1], step_s[m : m + 1]
            side_c.append(base_c * c - base_s * s)
            side_s.append(base_s * c + base_c * s)
        sides = jnp.concatenate(side_c + side_s, axis=0)
        sides_ref[b] = sides

        powers = [jnp.ones_like(t), t]
        for n in range(2, count):
            powers.append(2.0 * t * powers[-1] - powers[-2])
        powers = jnp.concatenate(powers, axis=0)
        powers_ref[b] = powers
        spread(count, powers, sides, high_ref.at[b], low_ref.at[b])

        heavy_high, heavy_low = split(phase * weight)
        both = jnp.concatenate([heavy_high, heavy_low], axis=0)
        across = (((1,), (1,)), ((), ()))
        first = lax.dot_general(both, high_ref[b], across, preferred_element_type=jnp.float32)
        second = lax.dot_general(heavy_high, low_ref[b], across, preferred_element_type=jnp.float32)
        moments = first[: 2 * PDIM] + first[2 * PDIM :] + second

        sums = [jnp.zeros(tile, jnp.float32) for _ in range(4)]
        for m in range(pairs):
            piece = moments[:, m * LANES : (m + 1) * LANES]
            for kind, values in enumerate((plus[m], minus[m])):
                sums[2 * kind] += values * piece[:PDIM]
                sums[2 * kind + 1] += values * piece[PDIM:]
        added = sums[0] + sign * roll(sums[1], LANES // 2)
        taken = roll(sums[3], LANES // 2) - sign * sums[2]
        found.append([swap_groups(v) + group_sign * v for v in (added, taken)])

    p, q_plus, q_minus = tile_orders()
    even = even_group(tile)
    for kind, order_q in enumerate((q_plus, q_minus)):
        wave_x, wave_y, wave_norm = wave(p, order_q, box_x, box_y)
        inverse = 1.0 / wave_norm
        unit_ref[kind, 0] = wave_x * inverse
        unit_ref[kind, 1] = wave_y * inverse
        boost = jnp.exp(wave_norm * height)
        prefix = [jnp.zeros(tile, jnp.float32)]
        for b in range(blocks):
            prefix.append(prefix[-1] + found[b][kind])
        total = prefix[-1]
        for b in range(blocks):
            before_ref[b, kind] = boost * jnp.where(even, prefix[b], total - prefix[b + 1])
        top, bottom = total[: PDIM // 2], total[PDIM // 2 :]
        small = even_group(top.shape)
        totals_ref[kind, 0] = jnp.where(small, top, roll(bottom, HALF))
        totals_ref[kind, 1] = jnp.where(small, roll(top, -HALF), bottom)
        depth = wave_norm * height
        decay_ref[kind] = jnp.where(small, depth[: PDIM // 2], depth[PDIM // 2 :])


def forces_kernel(
    count, carry_ref, unit_ref, before_ref, table_ref, weight_ref, phase_ref, sides_ref, powers_ref,
    forces_ref, coarse_ref, high_ref, low_ref,
):
    blocks = before_ref.shape[0]
    pairs = count // 2
    tile = (PDIM, LANES)
    sign = half_sign(tile)
    group_sign = jnp.where(even_group(tile), 1.0, -1.0)
    base = []
    small = even_group((PDIM // 2, LANES))
    for kind in range(2):
        up, down = carry_ref[kind, 0], carry_ref[kind, 1]
        top = jnp.where(small, up, roll(down, HALF))
        bottom = jnp.where(small, roll(up, -HALF), down)
        base.append(jnp.concatenate([top, bottom], axis=0))

    for b in range(blocks):
        span = slice(b * BLOCK, (b + 1) * BLOCK)
        sides = []
        for kind in range(2):
            held = base[kind] + before_ref[b, kind]
            mixed = held + group_sign * swap_groups(held)
            turned = sign * roll(mixed, LANES // 2)
            sides.append((unit_ref[kind, 0] * turned, unit_ref[kind, 1] * turned, -swap_groups(mixed)))
        for o in range(3):
            plus, minus = sides[0][o], sides[1][o]
            plus_rows = (plus, -sign * roll(plus, LANES // 2))
            minus_rows = (-sign * minus, roll(minus, LANES // 2))
            for m in range(pairs):
                lanes = slice(m * LANES, (m + 1) * LANES)
                table_plus = table_ref[0, :, lanes]
                table_minus = table_ref[1, :, lanes]
                for part in range(2):
                    at = (2 * o + part) * PDIM
                    high, low = split(table_plus * plus_rows[part] + table_minus * minus_rows[part])
                    coarse_ref[b, at : at + PDIM, lanes] = high
                    coarse_ref[b, 6 * PDIM + at : 6 * PDIM + at + PDIM, lanes] = low
        spread(count, powers_ref[b], sides_ref[b], high_ref.at[b], low_ref.at[b])
        field = jnp.dot(coarse_ref[b], high_ref[b], preferred_element_type=jnp.float32)
        field = field[: 6 * PDIM] + field[6 * PDIM :]
        field += jnp.dot(coarse_ref[b, : 6 * PDIM], low_ref[b], preferred_element_type=jnp.float32)
        phase = phase_ref[b]
        for o in range(3):
            part = field[o * 2 * PDIM : (o + 1) * 2 * PDIM]
            forces_ref[o : o + 1, span] = jnp.sum(phase * part, axis=0, keepdims=True) * weight_ref[0:1, span]


def doublings(first, size):
    return [first << i for i in range(32) if first << i < size]


def carries(totals, decay, slabs, modes):
    slab, mode = lax.axis_index("slab"), lax.axis_index("mode")
    part = jnp.arange(2, dtype=jnp.int32)[None, :, None, None]
    depth = decay[:, None]

    def swap(value, mask):
        return lax.ppermute(value, ("slab", "mode"), [(i, i ^ mask) for i in range(slabs * modes)])

    def ahead(rank, stride):
        return part != (rank // stride) % 2

    other = swap(totals, 1)
    inside = jnp.where(ahead(mode, 1), other, 0.0)
    totals = totals + other
    strides = doublings(2, modes)
    for stride in strides[:-1]:
        other = swap(totals, stride ^ 1)
        inside = inside + jnp.where(ahead(mode, stride), other, 0.0)
        totals = totals + other
    across, along, both = [swap(totals, mask) for mask in (strides[-1] ^ 1, modes ^ 1, modes ^ strides[-1] ^ 1)]
    inside = inside + jnp.where(ahead(mode, strides[-1]), across, 0.0)
    totals = totals + across
    other = along + both
    outside = jnp.exp(depth) * inside
    for stride in doublings(1, slabs):
        first = ahead(slab, stride)
        if stride > 1 and 2 * stride < slabs:
            other = swap(totals, (stride * modes) ^ 1)
        elif stride > 1:
            sent = jnp.where((slab // stride) % 2 == 0, totals[:, 0], totals[:, 1])
            other = swap(sent, (stride * modes) ^ 1)[:, None]
        below = slab % stride
        steps = jnp.where(part == 0, below, stride - 1 - below).astype(jnp.float32)
        outside = outside + jnp.where(first, other * jnp.exp(-depth * steps), 0.0)
        fade = jnp.exp(-depth * float(stride))
        totals = jnp.where(first, totals + fade * other, other + fade * totals)
    return outside


def shards(positions, charges, counts, box):
    slab_count = lax.axis_size("slab")
    mode_parts = lax.axis_size("mode")
    height = slab_span / slab_count
    count = series_terms(height)
    ions = positions.shape[1]
    blocks = ions // BLOCK
    terms = count * 2 * HALF
    half = PDIM // 2
    scalar = pl.BlockSpec(memory_space=pltpu.SMEM)
    vector = pl.BlockSpec(memory_space=pltpu.VMEM)
    params = pltpu.CompilerParams(vmem_limit_bytes=40 * 1024 * 1024)
    work = [pltpu.VMEM((blocks, terms, BLOCK), jnp.bfloat16)] * 2
    inputs = [
        pltpu.with_memory_space_constraint(v, pltpu.HBM) for v in (counts, box, positions, charges[None, :])
    ]
    totals, decay, *kept = pl.pallas_call(
        functools.partial(moments_kernel, count, height),
        out_shape=[
            pltpu.VMEM((2, 2, half, LANES), jnp.float32),
            pltpu.VMEM((2, half, LANES), jnp.float32),
            pltpu.VMEM((2, 2, PDIM, LANES), jnp.float32),
            pltpu.VMEM((blocks, 2, PDIM, LANES), jnp.float32),
            pltpu.VMEM((2, PDIM, terms), jnp.float32),
            pltpu.VMEM((1, ions), jnp.float32),
            pltpu.VMEM((blocks, 2 * PDIM, BLOCK), jnp.float32),
            pltpu.VMEM((blocks, 2 * HALF, BLOCK), jnp.float32),
            pltpu.VMEM((blocks, count, BLOCK), jnp.float32),
        ],
        in_specs=[scalar, scalar, vector, vector],
        out_specs=[vector] * 9,
        scratch_shapes=work,
        compiler_params=params,
        name="moments",
    )(*inputs)

    carry = carries(totals, decay, slab_count, mode_parts)

    carry, *kept = [pltpu.with_memory_space_constraint(v, pltpu.VMEM) for v in (carry, *kept)]
    return pl.pallas_call(
        functools.partial(forces_kernel, count),
        out_shape=jax.ShapeDtypeStruct((3, ions), jnp.float32),
        in_specs=[vector] * 8,
        out_specs=vector,
        scratch_shapes=[
            pltpu.VMEM((blocks, 12 * PDIM, terms), jnp.bfloat16),
        ] + work,
        compiler_params=params,
        name="forces",
    )(carry, *kept)


def solution(mesh):
    return jax.shard_map(
        shards,
        mesh=mesh,
        in_specs=(P(None, ("slab", "mode")), P(("slab", "mode")), P(), P()),
        out_specs=P(None, ("slab", "mode")),
        check_vma=False,
    )
```

```python
import functools
import math

import jax
import jax.numpy as jnp
import numpy as np
from jax import lax
from jax.experimental import pallas as pl
from jax.experimental.pallas import tpu as pltpu
from jax.sharding import PartitionSpec as P

QDIM = 64
BLOCK = 512
MODES = 4096
PDIM = MODES // QDIM
HALF = QDIM // 2
LANES = 4 * HALF

two_pi = 2.0 * math.pi
slab_span = 0.08
box_low = 0.8

SIN_TERMS = (3.14159264, -5.16771008, 2.55007752, -0.59829129, 0.07765766)
COS_TERMS = (1.0, -4.93480214, 4.05870916, -1.335212, 0.23493731, -0.02439632)


def series_terms(height):
    a = 0.5 * height * two_pi * math.hypot(PDIM, HALF) / box_low
    nodes = np.cos(np.pi * (np.arange(64) + 0.5) / 64)
    order = np.arange(32)[:, None]
    coefficients = np.abs((np.exp(-a * (1.0 + nodes)) * np.cos(order * np.arccos(nodes))).sum(1) / 32.0)
    count = 4
    while coefficients[count:].sum() > 2.0**-24:
        count += 4
    return count


def poly(terms, u):
    value = jnp.full_like(u, terms[-1])
    for term in terms[-2::-1]:
        value = value * u + term
    return value


def turn(angle):
    r = angle - jnp.floor(angle + 0.5)
    u = r * r
    s = r * poly(SIN_TERMS, u)
    c = poly(COS_TERMS, u)
    return 1.0 - 2.0 * s * s, 2.0 * s * c


def split(x):
    high = x.astype(jnp.bfloat16)
    return high, (x - high.astype(jnp.float32)).astype(jnp.bfloat16)


def iota(shape, dim):
    return lax.broadcasted_iota(jnp.int32, shape, dim)


def roll(x, shift):
    return pltpu.roll(x, shift % LANES, x.ndim - 1)


def even_group(shape):
    return (iota(shape, 1) // HALF) % 2 == 0


def swap_groups(x):
    return jnp.where(even_group(x.shape), roll(x, -HALF), roll(x, HALF))


def half_sign(shape):
    return jnp.where(iota(shape, 1) < LANES // 2, -1.0, 1.0)


def wave(order_p, order_q, box_x, box_y):
    wave_x = two_pi * order_p / box_x
    wave_y = two_pi * order_q / box_y
    return wave_x, wave_y, jnp.sqrt(wave_x * wave_x + wave_y * wave_y)


def tile_orders():
    shape = (PDIM, LANES)
    p = (iota(shape, 0) + 1).astype(jnp.float32)
    j = iota(shape, 1) % HALF
    return p, j.astype(jnp.float32), (-1 - j).astype(jnp.float32)


def table_terms(count, height, box_x, box_y):
    p, q_plus, q_minus = tile_orders()
    even = even_group(p.shape)
    a = (0.5 * height) * wave(p, jnp.where(even, q_plus, q_minus), box_x, box_y)[2]
    square = 0.25 * a * a
    last = count + 8
    scaled = {last + 1: jnp.ones_like(a), last: jnp.ones_like(a)}
    for n in range(last, 0, -1):
        scaled[n - 1] = scaled[n] + square * (scaled[n + 1] * (1.0 / (n * (n + 1))))
    power, total = jnp.ones_like(a), scaled[0]
    parts = [scaled[0]]
    for n in range(1, last + 1):
        power = power * (a * (0.5 / n))
        parts.append(2.0 * (power * scaled[n]))
        total = total + parts[n]
    first = 1.0 / total
    terms = [first * part for part in parts[:count]]
    plus, minus = [], []
    for m in range(count // 2):
        low, high = terms[2 * m], terms[2 * m + 1]
        plus.append(jnp.where(even, low, roll(high, HALF)))
        minus.append(jnp.where(even, roll(low, -HALF), high))
    return plus, minus


def spread(count, powers, sides, high_ref, low_ref):
    for m in range(count // 2):
        for part in range(2):
            for parity in range(2):
                at = m * LANES + part * 2 * HALF + parity * HALF
                n = 2 * m + parity
                high, low = split(powers[n : n + 1] * sides[part * HALF : (part + 1) * HALF])
                high_ref[at : at + HALF] = high
                low_ref[at : at + HALF] = low


def moments_kernel(
    count, height, counts_ref, box_ref, positions_ref, charges_ref,
    totals_ref, decay_ref, unit_ref, before_ref, table_ref, weight_ref, phase_ref, sides_ref, powers_ref,
    high_ref, low_ref,
):
    ions = positions_ref.shape[1]
    blocks = ions // BLOCK
    pairs = count // 2
    slab_rank = lax.axis_index("slab")
    mode_rank = lax.axis_index("mode")
    box_x = jnp.full((1, 1), box_ref[0], jnp.float32)
    box_y = jnp.full((1, 1), box_ref[1], jnp.float32)
    live = counts_ref[slab_rank]
    lower_edge = slab_rank.astype(jnp.float32) * height
    scale = (2.0 * two_pi) / (box_x * box_y)

    plus, minus = table_terms(count, height, box_x, box_y)
    for m in range(pairs):
        table_ref[0, :, m * LANES : (m + 1) * LANES] = plus[m]
        table_ref[1, :, m * LANES : (m + 1) * LANES] = minus[m]

    rows = iota((8, BLOCK), 0).astype(jnp.float32)
    upward, downward = [], []
    tile = (PDIM, LANES)
    sign = half_sign(tile)
    group_sign = jnp.where(even_group(tile), 1.0, -1.0)
    found = []
    for b in range(blocks):
        span = slice(b * BLOCK, (b + 1) * BLOCK)
        x = positions_ref[0:1, span]
        y = positions_ref[1:2, span]
        t = (positions_ref[2:3, span] - lower_edge) * (2.0 / height) - 1.0
        slot = mode_rank * ions + b * BLOCK + iota((1, BLOCK), 1)
        weight = jnp.where(slot < live, charges_ref[0:1, span], 0.0)
        weight_ref[0:1, span] = weight * scale

        x8 = 8.0 * x
        y8 = 8.0 * y
        x8 = x8 - jnp.floor(x8)
        y8 = y8 - jnp.floor(y8)
        base_c, base_s = turn((rows + 1.0) * x - 0.5 * y)
        step_c, step_s = turn(rows * x8)
        phase_c, phase_s = [base_c], [base_s]
        for m in range(1, PDIM // 8):
            c, s = step_c[m : m + 1], step_s[m : m + 1]
            phase_c.append(base_c * c - base_s * s)
            phase_s.append(base_s * c + base_c * s)
        phase = jnp.concatenate(phase_c + phase_s, axis=0)
        phase_ref[b] = phase
        base_c, base_s = turn((rows + 0.5) * y)
        step_c, step_s = turn(rows * y8)
        side_c, side_s = [base_c], [base_s]
        for m in range(1, HALF // 8):
            c, s = step_c[m : m + 1], step_s[m : m + 1]
            side_c.append(base_c * c - base_s * s)
            side_s.append(base_s * c + base_c * s)
        sides = jnp.concatenate(side_c + side_s, axis=0)
        sides_ref[b] = sides

        powers = [jnp.ones_like(t), t]
        for n in range(2, count):
            powers.append(2.0 * t * powers[-1] - powers[-2])
        powers = jnp.concatenate(powers, axis=0)
        powers_ref[b] = powers
        spread(count, powers, sides, high_ref.at[b], low_ref.at[b])

        heavy_high, heavy_low = split(phase * weight)
        both = jnp.concatenate([heavy_high, heavy_low], axis=0)
        across = (((1,), (1,)), ((), ()))
        first = lax.dot_general(both, high_ref[b], across, preferred_element_type=jnp.float32)
        second = lax.dot_general(heavy_high, low_ref[b], across, preferred_element_type=jnp.float32)
        moments = first[: 2 * PDIM] + first[2 * PDIM :] + second

        sums = [jnp.zeros(tile, jnp.float32) for _ in range(4)]
        for m in range(pairs):
            piece = moments[:, m * LANES : (m + 1) * LANES]
            for kind, values in enumerate((plus[m], minus[m])):
                sums[2 * kind] += values * piece[:PDIM]
                sums[2 * kind + 1] += values * piece[PDIM:]
        added = sums[0] + sign * roll(sums[1], LANES // 2)
        taken = roll(sums[3], LANES // 2) - sign * sums[2]
        found.append([swap_groups(v) + group_sign * v for v in (added, taken)])

    p, q_plus, q_minus = tile_orders()
    even = even_group(tile)
    for kind, order_q in enumerate((q_plus, q_minus)):
        wave_x, wave_y, wave_norm = wave(p, order_q, box_x, box_y)
        inverse = 1.0 / wave_norm
        unit_ref[kind, 0] = wave_x * inverse
        unit_ref[kind, 1] = wave_y * inverse
        boost = jnp.exp(wave_norm * height)
        prefix = [jnp.zeros(tile, jnp.float32)]
        for b in range(blocks):
            prefix.append(prefix[-1] + found[b][kind])
        total = prefix[-1]
        for b in range(blocks):
            before_ref[b, kind] = boost * jnp.where(even, prefix[b], total - prefix[b + 1])
        top, bottom = total[: PDIM // 2], total[PDIM // 2 :]
        small = even_group(top.shape)
        totals_ref[kind, 0] = jnp.where(small, top, roll(bottom, HALF))
        totals_ref[kind, 1] = jnp.where(small, roll(top, -HALF), bottom)
        depth = wave_norm * height
        decay_ref[kind] = jnp.where(small, depth[: PDIM // 2], depth[PDIM // 2 :])


def forces_kernel(
    count, carry_ref, unit_ref, before_ref, table_ref, weight_ref, phase_ref, sides_ref, powers_ref,
    forces_ref, coarse_ref, high_ref, low_ref,
):
    blocks = before_ref.shape[0]
    pairs = count // 2
    tile = (PDIM, LANES)
    sign = half_sign(tile)
    group_sign = jnp.where(even_group(tile), 1.0, -1.0)
    base = []
    small = even_group((PDIM // 2, LANES))
    for kind in range(2):
        up, down = carry_ref[kind, 0], carry_ref[kind, 1]
        top = jnp.where(small, up, roll(down, HALF))
        bottom = jnp.where(small, roll(up, -HALF), down)
        base.append(jnp.concatenate([top, bottom], axis=0))

    for b in range(blocks):
        span = slice(b * BLOCK, (b + 1) * BLOCK)
        sides = []
        for kind in range(2):
            held = base[kind] + before_ref[b, kind]
            mixed = held + group_sign * swap_groups(held)
            turned = sign * roll(mixed, LANES // 2)
            sides.append((unit_ref[kind, 0] * turned, unit_ref[kind, 1] * turned, -swap_groups(mixed)))
        for o in range(3):
            plus, minus = sides[0][o], sides[1][o]
            plus_rows = (plus, -sign * roll(plus, LANES // 2))
            minus_rows = (-sign * minus, roll(minus, LANES // 2))
            for m in range(pairs):
                lanes = slice(m * LANES, (m + 1) * LANES)
                table_plus = table_ref[0, :, lanes]
                table_minus = table_ref[1, :, lanes]
                for part in range(2):
                    at = (2 * o + part) * PDIM
                    high, low = split(table_plus * plus_rows[part] + table_minus * minus_rows[part])
                    coarse_ref[b, at : at + PDIM, lanes] = high
                    coarse_ref[b, 6 * PDIM + at : 6 * PDIM + at + PDIM, lanes] = low
        spread(count, powers_ref[b], sides_ref[b], high_ref.at[b], low_ref.at[b])
        field = jnp.dot(coarse_ref[b], high_ref[b], preferred_element_type=jnp.float32)
        field = field[: 6 * PDIM] + field[6 * PDIM :]
        field += jnp.dot(coarse_ref[b, : 6 * PDIM], low_ref[b], preferred_element_type=jnp.float32)
        phase = phase_ref[b]
        for o in range(3):
            part = field[o * 2 * PDIM : (o + 1) * 2 * PDIM]
            forces_ref[o : o + 1, span] = jnp.sum(phase * part, axis=0, keepdims=True) * weight_ref[0:1, span]


def doublings(first, size):
    return [first << i for i in range(32) if first << i < size]


def carries(totals, decay, slabs, modes):
    slab, mode = lax.axis_index("slab"), lax.axis_index("mode")
    part = jnp.arange(2, dtype=jnp.int32)[None, :, None, None]
    depth = decay[:, None]

    def swap(value, mask):
        return lax.ppermute(value, ("slab", "mode"), [(i, i ^ mask) for i in range(slabs * modes)])

    def ahead(rank, stride):
        return part != (rank // stride) % 2

    other = swap(totals, 1)
    inside = jnp.where(ahead(mode, 1), other, 0.0)
    totals = totals + other
    strides = doublings(2, modes)
    for stride in strides[:-1]:
        other = swap(totals, stride ^ 1)
        inside = inside + jnp.where(ahead(mode, stride), other, 0.0)
        totals = totals + other
    across, along, both = [swap(totals, mask) for mask in (strides[-1] ^ 1, modes ^ 1, modes ^ strides[-1] ^ 1)]
    inside = inside + jnp.where(ahead(mode, strides[-1]), across, 0.0)
    totals = totals + across
    other = along + both
    outside = jnp.exp(depth) * inside
    for stride in doublings(1, slabs // 4):
        first = ahead(slab, stride)
        if stride > 1:
            other = swap(totals, (stride * modes) ^ 1)
        below = slab % stride
        steps = jnp.where(part == 0, below, stride - 1 - below).astype(jnp.float32)
        outside = outside + jnp.where(first, other * jnp.exp(-depth * steps), 0.0)
        fade = jnp.exp(-depth * float(stride))
        totals = jnp.where(first, totals + fade * other, other + fade * totals)
    stride = slabs // 4
    group, below = slab // stride, slab % stride
    for mask in range(1, 4):
        partner = group ^ mask
        lower = partner < group
        sent = jnp.where(lower, totals[:, 1], totals[:, 0])
        other = swap(sent, (mask * stride * modes) ^ 1)[:, None]
        steps = jnp.where(lower, below, stride - 1 - below) + stride * (jnp.abs(group - partner) - 1)
        heard = other * jnp.exp(-depth * steps.astype(jnp.float32))
        outside = outside + jnp.where(part == jnp.where(lower, 0, 1), heard, 0.0)
    return outside


def shards(positions, charges, counts, box):
    slab_count = lax.axis_size("slab")
    mode_parts = lax.axis_size("mode")
    height = slab_span / slab_count
    count = series_terms(height)
    ions = positions.shape[1]
    blocks = ions // BLOCK
    terms = count * 2 * HALF
    half = PDIM // 2
    scalar = pl.BlockSpec(memory_space=pltpu.SMEM)
    vector = pl.BlockSpec(memory_space=pltpu.VMEM)
    params = pltpu.CompilerParams(vmem_limit_bytes=40 * 1024 * 1024)
    work = [pltpu.VMEM((blocks, terms, BLOCK), jnp.bfloat16)] * 2
    inputs = [
        pltpu.with_memory_space_constraint(v, pltpu.HBM) for v in (counts, box, positions, charges[None, :])
    ]
    totals, decay, *kept = pl.pallas_call(
        functools.partial(moments_kernel, count, height),
        out_shape=[
            pltpu.VMEM((2, 2, half, LANES), jnp.float32),
            pltpu.VMEM((2, half, LANES), jnp.float32),
            pltpu.VMEM((2, 2, PDIM, LANES), jnp.float32),
            pltpu.VMEM((blocks, 2, PDIM, LANES), jnp.float32),
            pltpu.VMEM((2, PDIM, terms), jnp.float32),
            pltpu.VMEM((1, ions), jnp.float32),
            pltpu.VMEM((blocks, 2 * PDIM, BLOCK), jnp.float32),
            pltpu.VMEM((blocks, 2 * HALF, BLOCK), jnp.float32),
            pltpu.VMEM((blocks, count, BLOCK), jnp.float32),
        ],
        in_specs=[scalar, scalar, vector, vector],
        out_specs=[vector] * 9,
        scratch_shapes=work,
        compiler_params=params,
        name="moments",
    )(*inputs)

    carry = carries(totals, decay, slab_count, mode_parts)

    carry, *kept = [pltpu.with_memory_space_constraint(v, pltpu.VMEM) for v in (carry, *kept)]
    return pl.pallas_call(
        functools.partial(forces_kernel, count),
        out_shape=jax.ShapeDtypeStruct((3, ions), jnp.float32),
        in_specs=[vector] * 8,
        out_specs=vector,
        scratch_shapes=[
            pltpu.VMEM((blocks, 12 * PDIM, terms), jnp.bfloat16),
        ] + work,
        compiler_params=params,
        name="forces",
    )(carry, *kept)


def solution(mesh):
    return jax.shard_map(
        shards,
        mesh=mesh,
        in_specs=(P(None, ("slab", "mode")), P(("slab", "mode")), P(), P()),
        out_specs=P(None, ("slab", "mode")),
        check_vma=False,
    )
```

```python
import functools
import math

import jax
import jax.numpy as jnp
import numpy as np
from jax import lax
from jax.experimental import pallas as pl
from jax.experimental.pallas import tpu as pltpu
from jax.sharding import PartitionSpec as P

QDIM = 64
BLOCK = 512
MODES = 4096
PDIM = MODES // QDIM
HALF = QDIM // 2
LANES = 4 * HALF

two_pi = 2.0 * math.pi
slab_span = 0.08
box_low = 0.8

SIN_TERMS = (3.14159264, -5.16771008, 2.55007752, -0.59829129, 0.07765766)
COS_TERMS = (1.0, -4.93480214, 4.05870916, -1.335212, 0.23493731, -0.02439632)


def series_terms(height):
    a = 0.5 * height * two_pi * math.hypot(PDIM, HALF) / box_low
    nodes = np.cos(np.pi * (np.arange(64) + 0.5) / 64)
    order = np.arange(32)[:, None]
    coefficients = np.abs((np.exp(-a * (1.0 + nodes)) * np.cos(order * np.arccos(nodes))).sum(1) / 32.0)
    count = 4
    while coefficients[count:].sum() > 2.0**-24:
        count += 4
    return count


def poly(terms, u):
    value = jnp.full_like(u, terms[-1])
    for term in terms[-2::-1]:
        value = value * u + term
    return value


def turn(angle):
    r = angle - jnp.floor(angle + 0.5)
    u = r * r
    s = r * poly(SIN_TERMS, u)
    c = poly(COS_TERMS, u)
    return 1.0 - 2.0 * s * s, 2.0 * s * c


def split(x):
    high = x.astype(jnp.bfloat16)
    return high, (x - high.astype(jnp.float32)).astype(jnp.bfloat16)


def iota(shape, dim):
    return lax.broadcasted_iota(jnp.int32, shape, dim)


def roll(x, shift):
    return pltpu.roll(x, shift % LANES, x.ndim - 1)


def even_group(shape):
    return (iota(shape, 1) // HALF) % 2 == 0


def swap_groups(x):
    return jnp.where(even_group(x.shape), roll(x, -HALF), roll(x, HALF))


def half_sign(shape):
    return jnp.where(iota(shape, 1) < LANES // 2, -1.0, 1.0)


def wave(order_p, order_q, box_x, box_y):
    wave_x = two_pi * order_p / box_x
    wave_y = two_pi * order_q / box_y
    return wave_x, wave_y, jnp.sqrt(wave_x * wave_x + wave_y * wave_y)


def tile_orders():
    shape = (PDIM, LANES)
    p = (iota(shape, 0) + 1).astype(jnp.float32)
    j = iota(shape, 1) % HALF
    return p, j.astype(jnp.float32), (-1 - j).astype(jnp.float32)


def table_terms(count, height, box_x, box_y):
    p, q_plus, q_minus = tile_orders()
    even = even_group(p.shape)
    a = (0.5 * height) * wave(p, jnp.where(even, q_plus, q_minus), box_x, box_y)[2]
    square = 0.25 * a * a
    last = count + 8
    scaled = {last + 1: jnp.ones_like(a), last: jnp.ones_like(a)}
    for n in range(last, 0, -1):
        scaled[n - 1] = scaled[n] + square * (scaled[n + 1] * (1.0 / (n * (n + 1))))
    power, total = jnp.ones_like(a), scaled[0]
    parts = [scaled[0]]
    for n in range(1, last + 1):
        power = power * (a * (0.5 / n))
        parts.append(2.0 * (power * scaled[n]))
        total = total + parts[n]
    first = 1.0 / total
    terms = [first * part for part in parts[:count]]
    plus, minus = [], []
    for m in range(count // 2):
        low, high = terms[2 * m], terms[2 * m + 1]
        plus.append(jnp.where(even, low, roll(high, HALF)))
        minus.append(jnp.where(even, roll(low, -HALF), high))
    return plus, minus


def spread(count, powers, sides, high_ref, low_ref):
    for m in range(count // 2):
        for part in range(2):
            for parity in range(2):
                at = m * LANES + part * 2 * HALF + parity * HALF
                n = 2 * m + parity
                high, low = split(powers[n : n + 1] * sides[part * HALF : (part + 1) * HALF])
                high_ref[at : at + HALF] = high
                low_ref[at : at + HALF] = low


def coefficients(pairs, held, unit_ref, table_ref, coarse_ref):
    tile = (PDIM, LANES)
    sign = half_sign(tile)
    group_sign = jnp.where(even_group(tile), 1.0, -1.0)
    sides = []
    for kind in range(2):
        mixed = held[kind] + group_sign * swap_groups(held[kind])
        turned = sign * roll(mixed, LANES // 2)
        sides.append((unit_ref[kind, 0] * turned, unit_ref[kind, 1] * turned, -swap_groups(mixed)))
    for o in range(3):
        plus, minus = sides[0][o], sides[1][o]
        plus_rows = (plus, -sign * roll(plus, LANES // 2))
        minus_rows = (-sign * minus, roll(minus, LANES // 2))
        for m in range(pairs):
            lanes = slice(m * LANES, (m + 1) * LANES)
            table_plus = table_ref[0, :, lanes]
            table_minus = table_ref[1, :, lanes]
            for part in range(2):
                at = (2 * o + part) * PDIM
                high, low = split(table_plus * plus_rows[part] + table_minus * minus_rows[part])
                coarse_ref[at : at + PDIM, lanes] = high
                coarse_ref[6 * PDIM + at : 6 * PDIM + at + PDIM, lanes] = low


def fields(coarse_ref, high_ref, low_ref, phase):
    field = jnp.dot(coarse_ref[...], high_ref[...], preferred_element_type=jnp.float32)
    field = field[: 6 * PDIM] + field[6 * PDIM :]
    field += jnp.dot(coarse_ref[: 6 * PDIM], low_ref[...], preferred_element_type=jnp.float32)
    parts = [field[o * 2 * PDIM : (o + 1) * 2 * PDIM] for o in range(3)]
    return jnp.concatenate([jnp.sum(phase * part, axis=0, keepdims=True) for part in parts], axis=0)


def moments_kernel(
    count, height, counts_ref, box_ref, positions_ref, charges_ref,
    totals_ref, decay_ref, unit_ref, before_ref, table_ref, weight_ref, phase_ref, sides_ref, powers_ref,
    high_ref, low_ref,
):
    ions = positions_ref.shape[1]
    blocks = ions // BLOCK
    pairs = count // 2
    slab_rank = lax.axis_index("slab")
    mode_rank = lax.axis_index("mode")
    box_x = jnp.full((1, 1), box_ref[0], jnp.float32)
    box_y = jnp.full((1, 1), box_ref[1], jnp.float32)
    live = counts_ref[slab_rank]
    lower_edge = slab_rank.astype(jnp.float32) * height
    scale = (2.0 * two_pi) / (box_x * box_y)

    plus, minus = table_terms(count, height, box_x, box_y)
    for m in range(pairs):
        table_ref[0, :, m * LANES : (m + 1) * LANES] = plus[m]
        table_ref[1, :, m * LANES : (m + 1) * LANES] = minus[m]

    rows = iota((8, BLOCK), 0).astype(jnp.float32)
    upward, downward = [], []
    tile = (PDIM, LANES)
    sign = half_sign(tile)
    group_sign = jnp.where(even_group(tile), 1.0, -1.0)
    found = []
    for b in range(blocks):
        span = slice(b * BLOCK, (b + 1) * BLOCK)
        x = positions_ref[0:1, span]
        y = positions_ref[1:2, span]
        t = (positions_ref[2:3, span] - lower_edge) * (2.0 / height) - 1.0
        slot = mode_rank * ions + b * BLOCK + iota((1, BLOCK), 1)
        weight = jnp.where(slot < live, charges_ref[0:1, span], 0.0)
        weight_ref[0:1, span] = weight * scale

        x8 = 8.0 * x
        y8 = 8.0 * y
        x8 = x8 - jnp.floor(x8)
        y8 = y8 - jnp.floor(y8)
        base_c, base_s = turn((rows + 1.0) * x - 0.5 * y)
        step_c, step_s = turn(rows * x8)
        phase_c, phase_s = [base_c], [base_s]
        for m in range(1, PDIM // 8):
            c, s = step_c[m : m + 1], step_s[m : m + 1]
            phase_c.append(base_c * c - base_s * s)
            phase_s.append(base_s * c + base_c * s)
        phase = jnp.concatenate(phase_c + phase_s, axis=0)
        phase_ref[b] = phase
        base_c, base_s = turn((rows + 0.5) * y)
        step_c, step_s = turn(rows * y8)
        side_c, side_s = [base_c], [base_s]
        for m in range(1, HALF // 8):
            c, s = step_c[m : m + 1], step_s[m : m + 1]
            side_c.append(base_c * c - base_s * s)
            side_s.append(base_s * c + base_c * s)
        sides = jnp.concatenate(side_c + side_s, axis=0)
        sides_ref[b] = sides

        powers = [jnp.ones_like(t), t]
        for n in range(2, count):
            powers.append(2.0 * t * powers[-1] - powers[-2])
        powers = jnp.concatenate(powers, axis=0)
        powers_ref[b] = powers
        spread(count, powers, sides, high_ref.at[b], low_ref.at[b])

        heavy_high, heavy_low = split(phase * weight)
        both = jnp.concatenate([heavy_high, heavy_low], axis=0)
        across = (((1,), (1,)), ((), ()))
        first = lax.dot_general(both, high_ref[b], across, preferred_element_type=jnp.float32)
        second = lax.dot_general(heavy_high, low_ref[b], across, preferred_element_type=jnp.float32)
        moments = first[: 2 * PDIM] + first[2 * PDIM :] + second

        sums = [jnp.zeros(tile, jnp.float32) for _ in range(4)]
        for m in range(pairs):
            piece = moments[:, m * LANES : (m + 1) * LANES]
            for kind, values in enumerate((plus[m], minus[m])):
                sums[2 * kind] += values * piece[:PDIM]
                sums[2 * kind + 1] += values * piece[PDIM:]
        added = sums[0] + sign * roll(sums[1], LANES // 2)
        taken = roll(sums[3], LANES // 2) - sign * sums[2]
        found.append([swap_groups(v) + group_sign * v for v in (added, taken)])

    p, q_plus, q_minus = tile_orders()
    even = even_group(tile)
    for kind, order_q in enumerate((q_plus, q_minus)):
        wave_x, wave_y, wave_norm = wave(p, order_q, box_x, box_y)
        inverse = 1.0 / wave_norm
        unit_ref[kind, 0] = wave_x * inverse
        unit_ref[kind, 1] = wave_y * inverse
        boost = jnp.exp(wave_norm * height)
        prefix = [jnp.zeros(tile, jnp.float32)]
        for b in range(blocks):
            prefix.append(prefix[-1] + found[b][kind])
        total = prefix[-1]
        for b in range(blocks):
            before_ref[b, kind] = boost * jnp.where(even, prefix[b], total - prefix[b + 1])
        top, bottom = total[: PDIM // 2], total[PDIM // 2 :]
        small = even_group(top.shape)
        totals_ref[kind, 0] = jnp.where(small, top, roll(bottom, HALF))
        totals_ref[kind, 1] = jnp.where(small, roll(top, -HALF), bottom)
        depth = wave_norm * height
        decay_ref[kind] = jnp.where(small, depth[: PDIM // 2], depth[PDIM // 2 :])


def near_kernel(
    count, chosen, before_ref, unit_ref, table_ref, phase_ref, sides_ref, powers_ref,
    forces_ref, coarse_ref, high_ref, low_ref,
):
    for i, b in enumerate(chosen):
        held = [before_ref[b, kind] for kind in range(2)]
        coefficients(count // 2, held, unit_ref, table_ref, coarse_ref.at[i])
        spread(count, powers_ref[b], sides_ref[b], high_ref.at[i], low_ref.at[i])
        forces_ref[:, i * BLOCK : (i + 1) * BLOCK] = fields(coarse_ref.at[i], high_ref.at[i], low_ref.at[i], phase_ref[b])


def forces_kernel(
    count, carry_ref, early_ref, late_ref, unit_ref, table_ref, weight_ref, phase_ref, sides_ref, powers_ref,
    forces_ref, coarse_ref, high_ref, low_ref,
):
    blocks = phase_ref.shape[0]
    held = []
    small = even_group((PDIM // 2, LANES))
    for kind in range(2):
        up, down = carry_ref[kind, 0], carry_ref[kind, 1]
        top = jnp.where(small, up, roll(down, HALF))
        bottom = jnp.where(small, roll(up, -HALF), down)
        held.append(jnp.concatenate([top, bottom], axis=0))
    coefficients(count // 2, held, unit_ref, table_ref, coarse_ref)
    first = early_ref.shape[1] // BLOCK
    for b in range(blocks):
        span = slice(b * BLOCK, (b + 1) * BLOCK)
        spread(count, powers_ref[b], sides_ref[b], high_ref.at[b], low_ref.at[b])
        near_ref, at = (early_ref, b) if b < first else (late_ref, b - first)
        near = near_ref[:, at * BLOCK : (at + 1) * BLOCK]
        far = fields(coarse_ref, high_ref.at[b], low_ref.at[b], phase_ref[b])
        forces_ref[:, span] = (far + near) * weight_ref[0:1, span]


def doublings(first, size):
    return [first << i for i in range(32) if first << i < size]


def carries(totals, decay, slabs, modes, early, late):
    slab, mode = lax.axis_index("slab"), lax.axis_index("mode")
    part = jnp.arange(2, dtype=jnp.int32)[None, :, None, None]
    depth = decay[:, None]

    def swap(value, mask):
        return lax.ppermute(value, ("slab", "mode"), [(i, i ^ mask) for i in range(slabs * modes)])

    def ahead(rank, stride):
        return part != (rank // stride) % 2

    other = swap(totals, 1)
    inside = jnp.where(ahead(mode, 1), other, 0.0)
    totals = totals + other
    strides = doublings(2, modes)
    for stride in strides[:-1]:
        other = swap(totals, stride ^ 1)
        inside = inside + jnp.where(ahead(mode, stride), other, 0.0)
        totals = totals + other
    across, along, both = [swap(totals, mask) for mask in (strides[-1] ^ 1, modes ^ 1, modes ^ strides[-1] ^ 1)]
    near = early()
    inside = inside + jnp.where(ahead(mode, strides[-1]), across, 0.0)
    totals = totals + across
    other = along + both
    outside = jnp.exp(depth) * inside
    for stride in doublings(1, slabs // 4):
        first = ahead(slab, stride)
        if stride > 1:
            other = swap(totals, (stride * modes) ^ 1)
        below = slab % stride
        steps = jnp.where(part == 0, below, stride - 1 - below).astype(jnp.float32)
        outside = outside + jnp.where(first, other * jnp.exp(-depth * steps), 0.0)
        fade = jnp.exp(-depth * float(stride))
        totals = jnp.where(first, totals + fade * other, other + fade * totals)
    totals, near = lax.optimization_barrier((totals, near))
    near = near[0], late(near[1])
    stride = slabs // 4
    group, below = slab // stride, slab % stride
    for mask in range(1, 4):
        partner = group ^ mask
        lower = partner < group
        sent = jnp.where(lower, totals[:, 1], totals[:, 0])
        other = swap(sent, (mask * stride * modes) ^ 1)[:, None]
        steps = jnp.where(lower, below, stride - 1 - below) + stride * (jnp.abs(group - partner) - 1)
        heard = other * jnp.exp(-depth * steps.astype(jnp.float32))
        outside = outside + jnp.where(part == jnp.where(lower, 0, 1), heard, 0.0)
    return outside, near


def shards(positions, charges, counts, box):
    slab_count = lax.axis_size("slab")
    mode_parts = lax.axis_size("mode")
    height = slab_span / slab_count
    count = series_terms(height)
    ions = positions.shape[1]
    blocks = ions // BLOCK
    terms = count * 2 * HALF
    half = PDIM // 2
    scalar = pl.BlockSpec(memory_space=pltpu.SMEM)
    vector = pl.BlockSpec(memory_space=pltpu.VMEM)
    params = pltpu.CompilerParams(vmem_limit_bytes=40 * 1024 * 1024)
    work = [pltpu.VMEM((blocks, terms, BLOCK), jnp.bfloat16)] * 2
    inputs = [
        pltpu.with_memory_space_constraint(v, pltpu.HBM) for v in (counts, box, positions, charges[None, :])
    ]
    totals, decay, *kept = pl.pallas_call(
        functools.partial(moments_kernel, count, height),
        out_shape=[
            pltpu.VMEM((2, 2, half, LANES), jnp.float32),
            pltpu.VMEM((2, half, LANES), jnp.float32),
            pltpu.VMEM((2, 2, PDIM, LANES), jnp.float32),
            pltpu.VMEM((blocks, 2, PDIM, LANES), jnp.float32),
            pltpu.VMEM((2, PDIM, terms), jnp.float32),
            pltpu.VMEM((1, ions), jnp.float32),
            pltpu.VMEM((blocks, 2 * PDIM, BLOCK), jnp.float32),
            pltpu.VMEM((blocks, 2 * HALF, BLOCK), jnp.float32),
            pltpu.VMEM((blocks, count, BLOCK), jnp.float32),
        ],
        in_specs=[scalar, scalar, vector, vector],
        out_specs=[vector] * 9,
        scratch_shapes=work,
        compiler_params=params,
        name="moments",
    )(*inputs)

    fast = lambda values: [pltpu.with_memory_space_constraint(v, pltpu.VMEM) for v in values]
    unit, before, table, weight, phase, sides, powers = kept
    halves = [range(0, blocks // 2), range(blocks // 2, blocks)]

    def near(before, chosen):
        operands = fast((before, unit, table, phase, sides, powers))
        return pl.pallas_call(
            functools.partial(near_kernel, count, chosen),
            out_shape=pltpu.VMEM((3, len(chosen) * BLOCK), jnp.float32),
            in_specs=[vector] * 6,
            out_specs=vector,
            scratch_shapes=[
                pltpu.VMEM((len(chosen), 12 * PDIM, terms), jnp.bfloat16),
                pltpu.VMEM((len(chosen), terms, BLOCK), jnp.bfloat16),
                pltpu.VMEM((len(chosen), terms, BLOCK), jnp.bfloat16),
            ],
            compiler_params=params,
            cost_estimate=pl.CostEstimate(flops=12 * PDIM * terms * BLOCK * len(chosen) * 3 // 2, bytes_accessed=1 << 20, transcendentals=0),
            name="near",
        )(*operands)

    carry, (early, late) = carries(
        totals, decay, slab_count, mode_parts,
        lambda: (near(before, halves[0]), before), lambda held: near(held, halves[1]),
    )
    return pl.pallas_call(
        functools.partial(forces_kernel, count),
        out_shape=jax.ShapeDtypeStruct((3, ions), jnp.float32),
        in_specs=[vector] * 9,
        out_specs=vector,
        scratch_shapes=[pltpu.VMEM((12 * PDIM, terms), jnp.bfloat16)] + work,
        compiler_params=params,
        name="forces",
    )(*fast((carry, early, late, unit, table, weight, phase, sides, powers)))


def solution(mesh):
    return jax.shard_map(
        shards,
        mesh=mesh,
        in_specs=(P(None, ("slab", "mode")), P(("slab", "mode")), P(), P()),
        out_specs=P(None, ("slab", "mode")),
        check_vma=False,
    )
```

```python
import functools
import math

import jax
import jax.numpy as jnp
import numpy as np
from jax import lax
from jax.experimental import pallas as pl
from jax.experimental.pallas import tpu as pltpu
from jax.sharding import PartitionSpec as P

QDIM = 64
BLOCK = 512
MODES = 4096
PDIM = MODES // QDIM
HALF = QDIM // 2
LANES = 4 * HALF

two_pi = 2.0 * math.pi
slab_span = 0.08
box_low = 0.8

SIN_TERMS = (3.14159264, -5.16771008, 2.55007752, -0.59829129, 0.07765766)
COS_TERMS = (1.0, -4.93480214, 4.05870916, -1.335212, 0.23493731, -0.02439632)


def series_terms(height):
    a = 0.5 * height * two_pi * math.hypot(PDIM, HALF) / box_low
    nodes = np.cos(np.pi * (np.arange(64) + 0.5) / 64)
    order = np.arange(32)[:, None]
    parts = np.abs((np.exp(-a * (1.0 + nodes)) * np.cos(order * np.arccos(nodes))).sum(1) / 32.0)
    parts[0] *= 0.5
    count = exact = 4
    while parts[count:].sum() > 2.0**-24:
        count += 4
    while exact < count and parts[exact:].max() > 2.0**-9 * parts.max():
        exact += 4
    return count, exact


def poly(terms, u):
    value = jnp.full_like(u, terms[-1])
    for term in terms[-2::-1]:
        value = value * u + term
    return value


def turn(angle):
    r = angle - jnp.floor(angle + 0.5)
    u = r * r
    s = r * poly(SIN_TERMS, u)
    c = poly(COS_TERMS, u)
    return 1.0 - 2.0 * s * s, 2.0 * s * c


def split(x):
    high = x.astype(jnp.bfloat16)
    return high, (x - high.astype(jnp.float32)).astype(jnp.bfloat16)


def iota(shape, dim):
    return lax.broadcasted_iota(jnp.int32, shape, dim)


def roll(x, shift):
    return pltpu.roll(x, shift % LANES, x.ndim - 1)


def even_group(shape):
    return (iota(shape, 1) // HALF) % 2 == 0


def swap_groups(x):
    return jnp.where(even_group(x.shape), roll(x, -HALF), roll(x, HALF))


def half_sign(shape):
    return jnp.where(iota(shape, 1) < LANES // 2, -1.0, 1.0)


def wave(order_p, order_q, box_x, box_y):
    wave_x = two_pi * order_p / box_x
    wave_y = two_pi * order_q / box_y
    return wave_x, wave_y, jnp.sqrt(wave_x * wave_x + wave_y * wave_y)


def tile_orders():
    shape = (PDIM, LANES)
    p = (iota(shape, 0) + 1).astype(jnp.float32)
    j = iota(shape, 1) % HALF
    return p, j.astype(jnp.float32), (-1 - j).astype(jnp.float32)


def table_terms(count, height, box_x, box_y):
    p, q_plus, q_minus = tile_orders()
    even = even_group(p.shape)
    a = (0.5 * height) * wave(p, jnp.where(even, q_plus, q_minus), box_x, box_y)[2]
    square = 0.25 * a * a
    last = count + 8
    scaled = {last + 1: jnp.ones_like(a), last: jnp.ones_like(a)}
    for n in range(last, 0, -1):
        scaled[n - 1] = scaled[n] + square * (scaled[n + 1] * (1.0 / (n * (n + 1))))
    power, total = jnp.ones_like(a), scaled[0]
    parts = [scaled[0]]
    for n in range(1, last + 1):
        power = power * (a * (0.5 / n))
        parts.append(2.0 * (power * scaled[n]))
        total = total + parts[n]
    first = 1.0 / total
    terms = [first * part for part in parts[:count]]
    plus, minus = [], []
    for m in range(count // 2):
        low, high = terms[2 * m], terms[2 * m + 1]
        plus.append(jnp.where(even, low, roll(high, HALF)))
        minus.append(jnp.where(even, roll(low, -HALF), high))
    return plus, minus


def spread(count, exact, powers, sides, spread_ref):
    for m in range(count // 2):
        for part in range(2):
            for parity in range(2):
                at = m * LANES + part * 2 * HALF + parity * HALF
                n = 2 * m + parity
                value = powers[n : n + 1] * sides[part * HALF : (part + 1) * HALF]
                if n < exact:
                    value, low = split(value)
                    spread_ref[count * 2 * HALF + at : count * 2 * HALF + at + HALF] = low
                spread_ref[at : at + HALF] = value.astype(jnp.bfloat16)


def coefficients(count, exact, held, unit_ref, table_ref, coarse_ref):
    tile = (PDIM, LANES)
    sign = half_sign(tile)
    group_sign = jnp.where(even_group(tile), 1.0, -1.0)
    sides = []
    for kind in range(2):
        mixed = held[kind] + group_sign * swap_groups(held[kind])
        turned = sign * roll(mixed, LANES // 2)
        sides.append((unit_ref[kind, 0] * turned, unit_ref[kind, 1] * turned, -swap_groups(mixed)))
    for o in range(3):
        plus, minus = sides[0][o], sides[1][o]
        plus_rows = (plus, -sign * roll(plus, LANES // 2))
        minus_rows = (-sign * minus, roll(minus, LANES // 2))
        for m in range(count // 2):
            lanes = slice(m * LANES, (m + 1) * LANES)
            table_plus = table_ref[0, :, lanes]
            table_minus = table_ref[1, :, lanes]
            for part in range(2):
                at = (2 * o + part) * PDIM
                value = table_plus * plus_rows[part] + table_minus * minus_rows[part]
                if 2 * m < exact:
                    value, low = split(value)
                    coarse_ref[6 * PDIM + at : 6 * PDIM + at + PDIM, lanes] = low
                    again = slice(count * 2 * HALF + m * LANES, count * 2 * HALF + (m + 1) * LANES)
                    coarse_ref[at : at + PDIM, again] = value
                coarse_ref[at : at + PDIM, lanes] = value.astype(jnp.bfloat16)


def fields(exact, coarse_ref, spread_ref, phase):
    cut = exact * 2 * HALF
    field = jnp.dot(coarse_ref[:, :cut], spread_ref[:cut], preferred_element_type=jnp.float32)
    field = field[: 6 * PDIM] + field[6 * PDIM :]
    field += jnp.dot(coarse_ref[: 6 * PDIM, cut:], spread_ref[cut:], preferred_element_type=jnp.float32)
    parts = [field[o * 2 * PDIM : (o + 1) * 2 * PDIM] for o in range(3)]
    return jnp.concatenate([jnp.sum(phase * part, axis=0, keepdims=True) for part in parts], axis=0)


def moments_kernel(
    count, exact, height, counts_ref, box_ref, positions_ref, charges_ref,
    totals_ref, decay_ref, unit_ref, before_ref, table_ref, weight_ref, phase_ref, sides_ref, powers_ref,
    spread_ref,
):
    ions = positions_ref.shape[1]
    blocks = ions // BLOCK
    pairs = count // 2
    slab_rank = lax.axis_index("slab")
    mode_rank = lax.axis_index("mode")
    box_x = jnp.full((1, 1), box_ref[0], jnp.float32)
    box_y = jnp.full((1, 1), box_ref[1], jnp.float32)
    live = counts_ref[slab_rank]
    lower_edge = slab_rank.astype(jnp.float32) * height
    scale = (2.0 * two_pi) / (box_x * box_y)

    plus, minus = table_terms(count, height, box_x, box_y)
    for m in range(pairs):
        table_ref[0, :, m * LANES : (m + 1) * LANES] = plus[m]
        table_ref[1, :, m * LANES : (m + 1) * LANES] = minus[m]

    rows = iota((8, BLOCK), 0).astype(jnp.float32)
    upward, downward = [], []
    tile = (PDIM, LANES)
    sign = half_sign(tile)
    group_sign = jnp.where(even_group(tile), 1.0, -1.0)
    found = []
    for b in range(blocks):
        span = slice(b * BLOCK, (b + 1) * BLOCK)
        x = positions_ref[0:1, span]
        y = positions_ref[1:2, span]
        t = (positions_ref[2:3, span] - lower_edge) * (2.0 / height) - 1.0
        slot = mode_rank * ions + b * BLOCK + iota((1, BLOCK), 1)
        weight = jnp.where(slot < live, charges_ref[0:1, span], 0.0)
        weight_ref[0:1, span] = weight * scale

        x8 = 8.0 * x
        y8 = 8.0 * y
        x8 = x8 - jnp.floor(x8)
        y8 = y8 - jnp.floor(y8)
        base_c, base_s = turn((rows + 1.0) * x - 0.5 * y)
        step_c, step_s = turn(rows * x8)
        phase_c, phase_s = [base_c], [base_s]
        for m in range(1, PDIM // 8):
            c, s = step_c[m : m + 1], step_s[m : m + 1]
            phase_c.append(base_c * c - base_s * s)
            phase_s.append(base_s * c + base_c * s)
        phase = jnp.concatenate(phase_c + phase_s, axis=0)
        phase_ref[b] = phase
        base_c, base_s = turn((rows + 0.5) * y)
        step_c, step_s = turn(rows * y8)
        side_c, side_s = [base_c], [base_s]
        for m in range(1, HALF // 8):
            c, s = step_c[m : m + 1], step_s[m : m + 1]
            side_c.append(base_c * c - base_s * s)
            side_s.append(base_s * c + base_c * s)
        sides = jnp.concatenate(side_c + side_s, axis=0)
        sides_ref[b] = sides

        powers = [jnp.ones_like(t), t]
        for n in range(2, count):
            powers.append(2.0 * t * powers[-1] - powers[-2])
        powers = jnp.concatenate(powers, axis=0)
        powers_ref[b] = powers
        spread(count, exact, powers, sides, spread_ref.at[b])

        heavy_high, heavy_low = split(phase * weight)
        both = jnp.concatenate([heavy_high, heavy_low], axis=0)
        across = (((1,), (1,)), ((), ()))
        cut, rest = exact * 2 * HALF, (count - exact) * 2 * HALF
        first = lax.dot_general(both, spread_ref[b, :cut], across, preferred_element_type=jnp.float32)
        second = lax.dot_general(heavy_high, spread_ref[b, cut:], across, preferred_element_type=jnp.float32)
        moments = first[: 2 * PDIM] + first[2 * PDIM :] + second[:, rest:]
        moments = [moments[:, m * LANES : (m + 1) * LANES] for m in range(exact // 2)]
        moments += [second[:, m * LANES : (m + 1) * LANES] for m in range((count - exact) // 2)]

        sums = [jnp.zeros(tile, jnp.float32) for _ in range(4)]
        for m in range(pairs):
            piece = moments[m]
            for kind, values in enumerate((plus[m], minus[m])):
                sums[2 * kind] += values * piece[:PDIM]
                sums[2 * kind + 1] += values * piece[PDIM:]
        added = sums[0] + sign * roll(sums[1], LANES // 2)
        taken = roll(sums[3], LANES // 2) - sign * sums[2]
        found.append([swap_groups(v) + group_sign * v for v in (added, taken)])

    p, q_plus, q_minus = tile_orders()
    even = even_group(tile)
    for kind, order_q in enumerate((q_plus, q_minus)):
        wave_x, wave_y, wave_norm = wave(p, order_q, box_x, box_y)
        inverse = 1.0 / wave_norm
        unit_ref[kind, 0] = wave_x * inverse
        unit_ref[kind, 1] = wave_y * inverse
        boost = jnp.exp(wave_norm * height)
        prefix = [jnp.zeros(tile, jnp.float32)]
        for b in range(blocks):
            prefix.append(prefix[-1] + found[b][kind])
        total = prefix[-1]
        for b in range(blocks):
            before_ref[b, kind] = boost * jnp.where(even, prefix[b], total - prefix[b + 1])
        top, bottom = total[: PDIM // 2], total[PDIM // 2 :]
        small = even_group(top.shape)
        totals_ref[kind, 0] = jnp.where(small, top, roll(bottom, HALF))
        totals_ref[kind, 1] = jnp.where(small, roll(top, -HALF), bottom)
        depth = wave_norm * height
        decay_ref[kind] = jnp.where(small, depth[: PDIM // 2], depth[PDIM // 2 :])


def near_kernel(
    count, exact, chosen, before_ref, unit_ref, table_ref, phase_ref, sides_ref, powers_ref,
    forces_ref, coarse_ref, spread_ref,
):
    for i, b in enumerate(chosen):
        held = [before_ref[b, kind] for kind in range(2)]
        coefficients(count, exact, held, unit_ref, table_ref, coarse_ref.at[i])
        spread(count, exact, powers_ref[b], sides_ref[b], spread_ref.at[i])
        found = fields(exact, coarse_ref.at[i], spread_ref.at[i], phase_ref[b])
        forces_ref[:, i * BLOCK : (i + 1) * BLOCK] = found


def forces_kernel(
    count, exact, carry_ref, early_ref, late_ref, unit_ref, table_ref, weight_ref, phase_ref, sides_ref, powers_ref,
    forces_ref, coarse_ref, spread_ref,
):
    blocks = phase_ref.shape[0]
    held = []
    small = even_group((PDIM // 2, LANES))
    for kind in range(2):
        up, down = carry_ref[kind, 0], carry_ref[kind, 1]
        top = jnp.where(small, up, roll(down, HALF))
        bottom = jnp.where(small, roll(up, -HALF), down)
        held.append(jnp.concatenate([top, bottom], axis=0))
    coefficients(count, exact, held, unit_ref, table_ref, coarse_ref)
    first = early_ref.shape[1] // BLOCK
    for b in range(blocks):
        span = slice(b * BLOCK, (b + 1) * BLOCK)
        spread(count, exact, powers_ref[b], sides_ref[b], spread_ref.at[b])
        near_ref, at = (early_ref, b) if b < first else (late_ref, b - first)
        near = near_ref[:, at * BLOCK : (at + 1) * BLOCK]
        far = fields(exact, coarse_ref, spread_ref.at[b], phase_ref[b])
        forces_ref[:, span] = (far + near) * weight_ref[0:1, span]


def doublings(first, size):
    return [first << i for i in range(32) if first << i < size]


def carries(totals, decay, slabs, modes, early, late):
    slab, mode = lax.axis_index("slab"), lax.axis_index("mode")
    part = jnp.arange(2, dtype=jnp.int32)[None, :, None, None]
    depth = decay[:, None]

    def swap(value, mask):
        return lax.ppermute(value, ("slab", "mode"), [(i, i ^ mask) for i in range(slabs * modes)])

    def ahead(rank, stride):
        return part != (rank // stride) % 2

    other = swap(totals, 1)
    inside = jnp.where(ahead(mode, 1), other, 0.0)
    totals = totals + other
    strides = doublings(2, modes)
    for stride in strides[:-1]:
        other = swap(totals, stride ^ 1)
        inside = inside + jnp.where(ahead(mode, stride), other, 0.0)
        totals = totals + other
    across, along, both = [swap(totals, mask) for mask in (strides[-1] ^ 1, modes ^ 1, modes ^ strides[-1] ^ 1)]
    near = early()
    inside = inside + jnp.where(ahead(mode, strides[-1]), across, 0.0)
    totals = totals + across
    other = along + both
    outside = jnp.exp(depth) * inside
    for stride in doublings(1, slabs // 4):
        first = ahead(slab, stride)
        if stride > 1:
            other = swap(totals, (stride * modes) ^ 1)
        below = slab % stride
        steps = jnp.where(part == 0, below, stride - 1 - below).astype(jnp.float32)
        outside = outside + jnp.where(first, other * jnp.exp(-depth * steps), 0.0)
        fade = jnp.exp(-depth * float(stride))
        totals = jnp.where(first, totals + fade * other, other + fade * totals)
    totals, near = lax.optimization_barrier((totals, near))
    near = near[0], late(near[1])
    stride = slabs // 4
    group, below = slab // stride, slab % stride
    for mask in range(1, 4):
        partner = group ^ mask
        lower = partner < group
        sent = jnp.where(lower, totals[:, 1], totals[:, 0])
        other = swap(sent, (mask * stride * modes) ^ 1)[:, None]
        steps = jnp.where(lower, below, stride - 1 - below) + stride * (jnp.abs(group - partner) - 1)
        heard = other * jnp.exp(-depth * steps.astype(jnp.float32))
        outside = outside + jnp.where(part == jnp.where(lower, 0, 1), heard, 0.0)
    return outside, near


def shards(positions, charges, counts, box):
    slab_count = lax.axis_size("slab")
    mode_parts = lax.axis_size("mode")
    height = slab_span / slab_count
    count, exact = series_terms(height)
    ions = positions.shape[1]
    blocks = ions // BLOCK
    terms, all_terms = count * 2 * HALF, (count + exact) * 2 * HALF
    half = PDIM // 2
    scalar = pl.BlockSpec(memory_space=pltpu.SMEM)
    vector = pl.BlockSpec(memory_space=pltpu.VMEM)
    params = pltpu.CompilerParams(vmem_limit_bytes=40 * 1024 * 1024)
    work = [pltpu.VMEM((blocks, all_terms, BLOCK), jnp.bfloat16)]
    inputs = [
        pltpu.with_memory_space_constraint(v, pltpu.HBM) for v in (counts, box, positions, charges[None, :])
    ]
    totals, decay, *kept = pl.pallas_call(
        functools.partial(moments_kernel, count, exact, height),
        out_shape=[
            pltpu.VMEM((2, 2, half, LANES), jnp.float32),
            pltpu.VMEM((2, half, LANES), jnp.float32),
            pltpu.VMEM((2, 2, PDIM, LANES), jnp.float32),
            pltpu.VMEM((blocks, 2, PDIM, LANES), jnp.float32),
            pltpu.VMEM((2, PDIM, terms), jnp.float32),
            pltpu.VMEM((1, ions), jnp.float32),
            pltpu.VMEM((blocks, 2 * PDIM, BLOCK), jnp.float32),
            pltpu.VMEM((blocks, 2 * HALF, BLOCK), jnp.float32),
            pltpu.VMEM((blocks, count, BLOCK), jnp.float32),
        ],
        in_specs=[scalar, scalar, vector, vector],
        out_specs=[vector] * 9,
        scratch_shapes=work,
        compiler_params=params,
        name="moments",
    )(*inputs)

    fast = lambda values: [pltpu.with_memory_space_constraint(v, pltpu.VMEM) for v in values]
    unit, before, table, weight, phase, sides, powers = kept
    halves = [range(0, blocks // 2), range(blocks // 2, blocks)]

    def near(before, chosen):
        operands = fast((before, unit, table, phase, sides, powers))
        return pl.pallas_call(
            functools.partial(near_kernel, count, exact, chosen),
            out_shape=pltpu.VMEM((3, len(chosen) * BLOCK), jnp.float32),
            in_specs=[vector] * 6,
            out_specs=vector,
            scratch_shapes=[
                pltpu.VMEM((len(chosen), 12 * PDIM, all_terms), jnp.bfloat16),
                pltpu.VMEM((len(chosen), all_terms, BLOCK), jnp.bfloat16),
            ],
            compiler_params=params,
            cost_estimate=pl.CostEstimate(flops=12 * PDIM * terms * BLOCK * len(chosen) * 3 // 2, bytes_accessed=1 << 20, transcendentals=0),
            name="near",
        )(*operands)

    carry, (early, late) = carries(
        totals, decay, slab_count, mode_parts,
        lambda: (near(before, halves[0]), before), lambda held: near(held, halves[1]),
    )
    return pl.pallas_call(
        functools.partial(forces_kernel, count, exact),
        out_shape=jax.ShapeDtypeStruct((3, ions), jnp.float32),
        in_specs=[vector] * 9,
        out_specs=vector,
        scratch_shapes=[pltpu.VMEM((12 * PDIM, all_terms), jnp.bfloat16)] + work,
        compiler_params=params,
        name="forces",
    )(*fast((carry, early, late, unit, table, weight, phase, sides, powers)))


def solution(mesh):
    return jax.shard_map(
        shards,
        mesh=mesh,
        in_specs=(P(None, ("slab", "mode")), P(("slab", "mode")), P(), P()),
        out_specs=P(None, ("slab", "mode")),
        check_vma=False,
    )
```

```python
import functools
import math

import jax
import jax.numpy as jnp
import numpy as np
from jax import lax
from jax.experimental import pallas as pl
from jax.experimental.pallas import tpu as pltpu
from jax.sharding import PartitionSpec as P

QDIM = 64
BLOCK = 512
MODES = 4096
PDIM = MODES // QDIM
HALF = QDIM // 2
LANES = 4 * HALF

two_pi = 2.0 * math.pi
slab_span = 0.08
box_low = 0.8

SIN_TERMS = (3.14159264, -5.16771008, 2.55007752, -0.59829129, 0.07765766)
COS_TERMS = (1.0, -4.93480214, 4.05870916, -1.335212, 0.23493731, -0.02439632)


def series_terms(height):
    a = 0.5 * height * two_pi * math.hypot(PDIM, HALF) / box_low
    nodes = np.cos(np.pi * (np.arange(64) + 0.5) / 64)
    order = np.arange(32)[:, None]
    parts = np.abs((np.exp(-a * (1.0 + nodes)) * np.cos(order * np.arccos(nodes))).sum(1) / 32.0)
    parts[0] *= 0.5
    count = exact = 4
    while parts[count:].sum() > 2.0**-24:
        count += 4
    while exact < count and parts[exact:].max() > 2.0**-9 * parts.max():
        exact += 4
    return count, exact


def poly(terms, u):
    value = jnp.full_like(u, terms[-1])
    for term in terms[-2::-1]:
        value = value * u + term
    return value


def turn(angle):
    r = angle - jnp.floor(angle + 0.5)
    u = r * r
    s = r * poly(SIN_TERMS, u)
    c = poly(COS_TERMS, u)
    return 1.0 - 2.0 * s * s, 2.0 * s * c


def split(x):
    high = x.astype(jnp.bfloat16)
    return high, (x - high.astype(jnp.float32)).astype(jnp.bfloat16)


def iota(shape, dim):
    return lax.broadcasted_iota(jnp.int32, shape, dim)


def roll(x, shift):
    return pltpu.roll(x, shift % LANES, x.ndim - 1)


def even_group(shape):
    return (iota(shape, 1) // HALF) % 2 == 0


def swap_groups(x):
    return jnp.where(even_group(x.shape), roll(x, -HALF), roll(x, HALF))


def half_sign(shape):
    return jnp.where(iota(shape, 1) < LANES // 2, -1.0, 1.0)


def wave(order_p, order_q, box_x, box_y):
    wave_x = two_pi * order_p / box_x
    wave_y = two_pi * order_q / box_y
    return wave_x, wave_y, jnp.sqrt(wave_x * wave_x + wave_y * wave_y)


def tile_orders():
    shape = (PDIM, LANES)
    p = (iota(shape, 0) + 1).astype(jnp.float32)
    j = iota(shape, 1) % HALF
    return p, j.astype(jnp.float32), (-1 - j).astype(jnp.float32)


def table_terms(count, height, box_x, box_y):
    p, q_plus, q_minus = tile_orders()
    even = even_group(p.shape)
    a = (0.5 * height) * wave(p, jnp.where(even, q_plus, q_minus), box_x, box_y)[2]
    square = 0.25 * a * a
    last = count + 3
    scaled = {last + 1: jnp.ones_like(a), last: jnp.ones_like(a)}
    for n in range(last, 0, -1):
        scaled[n - 1] = scaled[n] + square * (scaled[n + 1] * (1.0 / (n * (n + 1))))
    power, total = jnp.ones_like(a), scaled[0]
    parts = [scaled[0]]
    for n in range(1, last + 1):
        power = power * (a * (0.5 / n))
        parts.append(2.0 * (power * scaled[n]))
        total = total + parts[n]
    first = 1.0 / total
    terms = [first * part for part in parts[:count]]
    plus, minus = [], []
    for m in range(count // 2):
        low, high = terms[2 * m], terms[2 * m + 1]
        plus.append(jnp.where(even, low, roll(high, HALF)))
        minus.append(jnp.where(even, roll(low, -HALF), high))
    return plus, minus


def spread(count, exact, powers, sides, spread_ref):
    for m in range(count // 2):
        for part in range(2):
            for parity in range(2):
                at = m * LANES + part * 2 * HALF + parity * HALF
                n = 2 * m + parity
                value = powers[n : n + 1] * sides[part * HALF : (part + 1) * HALF]
                if n < exact:
                    value, low = split(value)
                    spread_ref[count * 2 * HALF + at : count * 2 * HALF + at + HALF] = low
                spread_ref[at : at + HALF] = value.astype(jnp.bfloat16)


def coefficients(count, exact, held, unit_ref, table_ref, coarse_ref):
    tile = (PDIM, LANES)
    sign = half_sign(tile)
    group_sign = jnp.where(even_group(tile), 1.0, -1.0)
    sides = []
    for kind in range(2):
        mixed = held[kind] + group_sign * swap_groups(held[kind])
        turned = sign * roll(mixed, LANES // 2)
        sides.append((unit_ref[kind, 0] * turned, unit_ref[kind, 1] * turned, -swap_groups(mixed)))
    for o in range(3):
        plus, minus = sides[0][o], sides[1][o]
        plus_rows = (plus, -sign * roll(plus, LANES // 2))
        minus_rows = (-sign * minus, roll(minus, LANES // 2))
        for m in range(count // 2):
            lanes = slice(m * LANES, (m + 1) * LANES)
            table_plus = table_ref[0, :, lanes]
            table_minus = table_ref[1, :, lanes]
            for part in range(2):
                at = (2 * o + part) * PDIM
                value = table_plus * plus_rows[part] + table_minus * minus_rows[part]
                if 2 * m < exact:
                    value, low = split(value)
                    coarse_ref[6 * PDIM + at : 6 * PDIM + at + PDIM, lanes] = low
                    again = slice(count * 2 * HALF + m * LANES, count * 2 * HALF + (m + 1) * LANES)
                    coarse_ref[at : at + PDIM, again] = value
                coarse_ref[at : at + PDIM, lanes] = value.astype(jnp.bfloat16)


def fields(exact, coarse_ref, spread_ref, phase):
    cut = exact * 2 * HALF
    field = jnp.dot(coarse_ref[:, :cut], spread_ref[:cut], preferred_element_type=jnp.float32)
    field = field[: 6 * PDIM] + field[6 * PDIM :]
    field += jnp.dot(coarse_ref[: 6 * PDIM, cut:], spread_ref[cut:], preferred_element_type=jnp.float32)
    parts = [field[o * 2 * PDIM : (o + 1) * 2 * PDIM] for o in range(3)]
    return jnp.concatenate([jnp.sum(phase * part, axis=0, keepdims=True) for part in parts], axis=0)


def moments_kernel(
    count, exact, height, counts_ref, box_ref, positions_ref, charges_ref,
    totals_ref, decay_ref, unit_ref, before_ref, table_ref, weight_ref, phase_ref, sides_ref, powers_ref,
    spread_ref,
):
    ions = positions_ref.shape[1]
    blocks = ions // BLOCK
    pairs = count // 2
    slab_rank = lax.axis_index("slab")
    mode_rank = lax.axis_index("mode")
    box_x = jnp.full((1, 1), box_ref[0], jnp.float32)
    box_y = jnp.full((1, 1), box_ref[1], jnp.float32)
    live = counts_ref[slab_rank]
    lower_edge = slab_rank.astype(jnp.float32) * height
    scale = (2.0 * two_pi) / (box_x * box_y)

    plus, minus = table_terms(count, height, box_x, box_y)
    for m in range(pairs):
        table_ref[0, :, m * LANES : (m + 1) * LANES] = plus[m]
        table_ref[1, :, m * LANES : (m + 1) * LANES] = minus[m]

    rows = iota((8, BLOCK), 0).astype(jnp.float32)
    upward, downward = [], []
    tile = (PDIM, LANES)
    sign = half_sign(tile)
    group_sign = jnp.where(even_group(tile), 1.0, -1.0)
    found = []
    for b in range(blocks):
        span = slice(b * BLOCK, (b + 1) * BLOCK)
        x = positions_ref[0:1, span]
        y = positions_ref[1:2, span]
        t = (positions_ref[2:3, span] - lower_edge) * (2.0 / height) - 1.0
        slot = mode_rank * ions + b * BLOCK + iota((1, BLOCK), 1)
        weight = jnp.where(slot < live, charges_ref[0:1, span], 0.0)
        weight_ref[0:1, span] = weight * scale

        x8 = 8.0 * x
        y8 = 8.0 * y
        x8 = x8 - jnp.floor(x8)
        y8 = y8 - jnp.floor(y8)
        base_c, base_s = turn((rows + 1.0) * x - 0.5 * y)
        step_c, step_s = turn(rows * x8)
        phase_c, phase_s = [base_c], [base_s]
        for m in range(1, PDIM // 8):
            c, s = step_c[m : m + 1], step_s[m : m + 1]
            phase_c.append(base_c * c - base_s * s)
            phase_s.append(base_s * c + base_c * s)
        phase = jnp.concatenate(phase_c + phase_s, axis=0)
        phase_ref[b] = phase
        base_c, base_s = turn((rows + 0.5) * y)
        step_c, step_s = turn(rows * y8)
        side_c, side_s = [base_c], [base_s]
        for m in range(1, HALF // 8):
            c, s = step_c[m : m + 1], step_s[m : m + 1]
            side_c.append(base_c * c - base_s * s)
            side_s.append(base_s * c + base_c * s)
        sides = jnp.concatenate(side_c + side_s, axis=0)
        sides_ref[b] = sides

        powers = [jnp.ones_like(t), t]
        for n in range(2, count):
            powers.append(2.0 * t * powers[-1] - powers[-2])
        powers = jnp.concatenate(powers, axis=0)
        powers_ref[b] = powers
        spread(count, exact, powers, sides, spread_ref.at[b])

        heavy_high, heavy_low = split(phase * weight)
        both = jnp.concatenate([heavy_high, heavy_low], axis=0)
        across = (((1,), (1,)), ((), ()))
        cut, rest = exact * 2 * HALF, (count - exact) * 2 * HALF
        found_parts = lax.dot_general(both, spread_ref[b], across, preferred_element_type=jnp.float32)
        second = found_parts[: 2 * PDIM] + found_parts[2 * PDIM :]
        moments = second[:, :cut] + found_parts[: 2 * PDIM, cut + rest :]
        second = second[:, cut : cut + rest]
        moments = [moments[:, m * LANES : (m + 1) * LANES] for m in range(exact // 2)]
        moments += [second[:, m * LANES : (m + 1) * LANES] for m in range((count - exact) // 2)]

        sums = [jnp.zeros(tile, jnp.float32) for _ in range(4)]
        for m in range(pairs):
            piece = moments[m]
            for kind, values in enumerate((plus[m], minus[m])):
                sums[2 * kind] += values * piece[:PDIM]
                sums[2 * kind + 1] += values * piece[PDIM:]
        added = sums[0] + sign * roll(sums[1], LANES // 2)
        taken = roll(sums[3], LANES // 2) - sign * sums[2]
        found.append([swap_groups(v) + group_sign * v for v in (added, taken)])

    p, q_plus, q_minus = tile_orders()
    even = even_group(tile)
    for kind, order_q in enumerate((q_plus, q_minus)):
        wave_x, wave_y, wave_norm = wave(p, order_q, box_x, box_y)
        inverse = 1.0 / wave_norm
        unit_ref[kind, 0] = wave_x * inverse
        unit_ref[kind, 1] = wave_y * inverse
        boost = jnp.exp(wave_norm * height)
        prefix = [jnp.zeros(tile, jnp.float32)]
        for b in range(blocks):
            prefix.append(prefix[-1] + found[b][kind])
        total = prefix[-1]
        for b in range(blocks):
            before_ref[b, kind] = boost * jnp.where(even, prefix[b], total - prefix[b + 1])
        top, bottom = total[: PDIM // 2], total[PDIM // 2 :]
        small = even_group(top.shape)
        totals_ref[kind, 0] = jnp.where(small, top, roll(bottom, HALF))
        totals_ref[kind, 1] = jnp.where(small, roll(top, -HALF), bottom)
        depth = wave_norm * height
        decay_ref[kind] = jnp.where(small, depth[: PDIM // 2], depth[PDIM // 2 :])


def near_kernel(
    count, exact, chosen, before_ref, unit_ref, table_ref, phase_ref, sides_ref, powers_ref,
    forces_ref, coarse_ref, spread_ref,
):
    for i, b in enumerate(chosen):
        held = [before_ref[b, kind] for kind in range(2)]
        coefficients(count, exact, held, unit_ref, table_ref, coarse_ref.at[i])
        spread(count, exact, powers_ref[b], sides_ref[b], spread_ref.at[i])
        found = fields(exact, coarse_ref.at[i], spread_ref.at[i], phase_ref[b])
        forces_ref[:, i * BLOCK : (i + 1) * BLOCK] = found


def forces_kernel(
    count, exact, carry_ref, early_ref, late_ref, unit_ref, table_ref, weight_ref, phase_ref, sides_ref, powers_ref,
    forces_ref, coarse_ref, spread_ref,
):
    blocks = phase_ref.shape[0]
    held = []
    small = even_group((PDIM // 2, LANES))
    for kind in range(2):
        up, down = carry_ref[kind, 0], carry_ref[kind, 1]
        top = jnp.where(small, up, roll(down, HALF))
        bottom = jnp.where(small, roll(up, -HALF), down)
        held.append(jnp.concatenate([top, bottom], axis=0))
    coefficients(count, exact, held, unit_ref, table_ref, coarse_ref)
    first = early_ref.shape[1] // BLOCK
    for b in range(blocks):
        span = slice(b * BLOCK, (b + 1) * BLOCK)
        spread(count, exact, powers_ref[b], sides_ref[b], spread_ref.at[b])
        near_ref, at = (early_ref, b) if b < first else (late_ref, b - first)
        near = near_ref[:, at * BLOCK : (at + 1) * BLOCK]
        far = fields(exact, coarse_ref, spread_ref.at[b], phase_ref[b])
        forces_ref[:, span] = (far + near) * weight_ref[0:1, span]


def doublings(first, size):
    return [first << i for i in range(32) if first << i < size]


def carries(totals, decay, slabs, modes, early, late):
    slab, mode = lax.axis_index("slab"), lax.axis_index("mode")
    part = jnp.arange(2, dtype=jnp.int32)[None, :, None, None]
    depth = decay[:, None]

    def swap(value, mask):
        return lax.ppermute(value, ("slab", "mode"), [(i, i ^ mask) for i in range(slabs * modes)])

    def ahead(rank, stride):
        return part != (rank // stride) % 2

    other = swap(totals, 1)
    inside = jnp.where(ahead(mode, 1), other, 0.0)
    totals = totals + other
    strides = doublings(2, modes)
    for stride in strides[:-1]:
        other = swap(totals, stride ^ 1)
        inside = inside + jnp.where(ahead(mode, stride), other, 0.0)
        totals = totals + other
    across, both, along = [swap(totals, mask) for mask in (strides[-1] ^ 1, modes ^ strides[-1] ^ 1, modes ^ 1)]
    near = early()
    inside = inside + jnp.where(ahead(mode, strides[-1]), across, 0.0)
    totals = totals + across
    other = along + both
    outside = jnp.exp(depth) * inside
    for stride in doublings(1, slabs // 4):
        first = ahead(slab, stride)
        if stride > 1:
            other = swap(totals, (stride * modes) ^ 1)
        below = slab % stride
        steps = jnp.where(part == 0, below, stride - 1 - below).astype(jnp.float32)
        outside = outside + jnp.where(first, other * jnp.exp(-depth * steps), 0.0)
        fade = jnp.exp(-depth * float(stride))
        totals = jnp.where(first, totals + fade * other, other + fade * totals)
    totals, near = lax.optimization_barrier((totals, near))
    near = near[0], late(near[1])
    stride = slabs // 4
    group, below = slab // stride, slab % stride
    for mask in range(1, 4):
        partner = group ^ mask
        lower = partner < group
        sent = jnp.where(lower, totals[:, 1], totals[:, 0])
        other = swap(sent, (mask * stride * modes) ^ 1)[:, None]
        steps = jnp.where(lower, below, stride - 1 - below) + stride * (jnp.abs(group - partner) - 1)
        heard = other * jnp.exp(-depth * steps.astype(jnp.float32))
        outside = outside + jnp.where(part == jnp.where(lower, 0, 1), heard, 0.0)
    return outside, near


def shards(positions, charges, counts, box):
    slab_count = lax.axis_size("slab")
    mode_parts = lax.axis_size("mode")
    height = slab_span / slab_count
    count, exact = series_terms(height)
    ions = positions.shape[1]
    blocks = ions // BLOCK
    terms, all_terms = count * 2 * HALF, (count + exact) * 2 * HALF
    half = PDIM // 2
    scalar = pl.BlockSpec(memory_space=pltpu.SMEM)
    vector = pl.BlockSpec(memory_space=pltpu.VMEM)
    params = pltpu.CompilerParams(vmem_limit_bytes=40 * 1024 * 1024)
    work = [pltpu.VMEM((blocks, all_terms, BLOCK), jnp.bfloat16)]
    inputs = [
        pltpu.with_memory_space_constraint(v, pltpu.HBM) for v in (counts, box, positions, charges[None, :])
    ]
    totals, decay, *kept = pl.pallas_call(
        functools.partial(moments_kernel, count, exact, height),
        out_shape=[
            pltpu.VMEM((2, 2, half, LANES), jnp.float32),
            pltpu.VMEM((2, half, LANES), jnp.float32),
            pltpu.VMEM((2, 2, PDIM, LANES), jnp.float32),
            pltpu.VMEM((blocks, 2, PDIM, LANES), jnp.float32),
            pltpu.VMEM((2, PDIM, terms), jnp.float32),
            pltpu.VMEM((1, ions), jnp.float32),
            pltpu.VMEM((blocks, 2 * PDIM, BLOCK), jnp.float32),
            pltpu.VMEM((blocks, 2 * HALF, BLOCK), jnp.float32),
            pltpu.VMEM((blocks, count, BLOCK), jnp.float32),
        ],
        in_specs=[scalar, scalar, vector, vector],
        out_specs=[vector] * 9,
        scratch_shapes=work,
        compiler_params=params,
        name="moments",
    )(*inputs)

    fast = lambda values: [pltpu.with_memory_space_constraint(v, pltpu.VMEM) for v in values]
    unit, before, table, weight, phase, sides, powers = kept
    halves = [range(0, blocks // 2), range(blocks // 2, blocks)]

    def near(before, chosen):
        operands = fast((before, unit, table, phase, sides, powers))
        return pl.pallas_call(
            functools.partial(near_kernel, count, exact, chosen),
            out_shape=pltpu.VMEM((3, len(chosen) * BLOCK), jnp.float32),
            in_specs=[vector] * 6,
            out_specs=vector,
            scratch_shapes=[
                pltpu.VMEM((len(chosen), 12 * PDIM, all_terms), jnp.bfloat16),
                pltpu.VMEM((len(chosen), all_terms, BLOCK), jnp.bfloat16),
            ],
            compiler_params=params,
            cost_estimate=pl.CostEstimate(flops=12 * PDIM * terms * BLOCK * len(chosen) * 3 // 2, bytes_accessed=1 << 20, transcendentals=0),
            name="near",
        )(*operands)

    carry, (early, late) = carries(
        totals, decay, slab_count, mode_parts,
        lambda: (near(before, halves[0]), before), lambda held: near(held, halves[1]),
    )
    return pl.pallas_call(
        functools.partial(forces_kernel, count, exact),
        out_shape=jax.ShapeDtypeStruct((3, ions), jnp.float32),
        in_specs=[vector] * 9,
        out_specs=vector,
        scratch_shapes=[pltpu.VMEM((12 * PDIM, all_terms), jnp.bfloat16)] + work,
        compiler_params=params,
        name="forces",
    )(*fast((carry, early, late, unit, table, weight, phase, sides, powers)))


def solution(mesh):
    return jax.shard_map(
        shards,
        mesh=mesh,
        in_specs=(P(None, ("slab", "mode")), P(("slab", "mode")), P(), P()),
        out_specs=P(None, ("slab", "mode")),
        check_vma=False,
    )
```

```python
import functools
import math

import jax
import jax.numpy as jnp
import numpy as np
from jax import lax
from jax.experimental import pallas as pl
from jax.experimental.pallas import tpu as pltpu
from jax.sharding import PartitionSpec as P

QDIM = 64
BLOCK = 512
MODES = 4096
PDIM = MODES // QDIM
HALF = QDIM // 2
LANES = 4 * HALF

two_pi = 2.0 * math.pi
slab_span = 0.08
box_low = 0.8

SIN_TERMS = (3.14159264, -5.16771008, 2.55007752, -0.59829129, 0.07765766)
COS_TERMS = (1.0, -4.93480214, 4.05870916, -1.335212, 0.23493731, -0.02439632)


def series_terms(height):
    a = 0.5 * height * two_pi * math.hypot(PDIM, HALF) / box_low
    nodes = np.cos(np.pi * (np.arange(64) + 0.5) / 64)
    order = np.arange(32)[:, None]
    parts = np.abs((np.exp(-a * (1.0 + nodes)) * np.cos(order * np.arccos(nodes))).sum(1) / 32.0)
    parts[0] *= 0.5
    count = exact = 4
    while parts[count:].sum() > 2.0**-24:
        count += 4
    while exact < count and parts[exact:].max() > 2.0**-9 * parts.max():
        exact += 4
    return count, exact


def poly(terms, u):
    value = jnp.full_like(u, terms[-1])
    for term in terms[-2::-1]:
        value = value * u + term
    return value


def turn(angle):
    r = angle - jnp.floor(angle + 0.5)
    u = r * r
    s = r * poly(SIN_TERMS, u)
    c = poly(COS_TERMS, u)
    return 1.0 - 2.0 * s * s, 2.0 * s * c


def split(x):
    high = x.astype(jnp.bfloat16)
    return high, (x - high.astype(jnp.float32)).astype(jnp.bfloat16)


def iota(shape, dim):
    return lax.broadcasted_iota(jnp.int32, shape, dim)


def roll(x, shift):
    return pltpu.roll(x, shift % LANES, x.ndim - 1)


def even_group(shape):
    return (iota(shape, 1) // HALF) % 2 == 0


def swap_groups(x):
    return jnp.where(even_group(x.shape), roll(x, -HALF), roll(x, HALF))


def half_sign(shape):
    return jnp.where(iota(shape, 1) < LANES // 2, -1.0, 1.0)


def wave(order_p, order_q, box_x, box_y):
    wave_x = two_pi * order_p / box_x
    wave_y = two_pi * order_q / box_y
    return wave_x, wave_y, jnp.sqrt(wave_x * wave_x + wave_y * wave_y)


def tile_orders():
    shape = (PDIM, LANES)
    p = (iota(shape, 0) + 1).astype(jnp.float32)
    j = iota(shape, 1) % HALF
    return p, j.astype(jnp.float32), (-1 - j).astype(jnp.float32)


def table_terms(count, height, box_x, box_y):
    p, q_plus, q_minus = tile_orders()
    even = even_group(p.shape)
    a = (0.5 * height) * wave(p, jnp.where(even, q_plus, q_minus), box_x, box_y)[2]
    square = 0.25 * a * a
    last = count + 3
    scaled = {last + 1: jnp.ones_like(a), last: jnp.ones_like(a)}
    for n in range(last, 0, -1):
        scaled[n - 1] = scaled[n] + square * (scaled[n + 1] * (1.0 / (n * (n + 1))))
    power, total = jnp.ones_like(a), scaled[0]
    parts = [scaled[0]]
    for n in range(1, last + 1):
        power = power * (a * (0.5 / n))
        parts.append(2.0 * (power * scaled[n]))
        total = total + parts[n]
    first = 1.0 / total
    terms = [first * part for part in parts[:count]]
    plus, minus = [], []
    for m in range(count // 2):
        low, high = terms[2 * m], terms[2 * m + 1]
        plus.append(jnp.where(even, low, roll(high, HALF)))
        minus.append(jnp.where(even, roll(low, -HALF), high))
    return plus, minus


def spread(count, exact, powers, sides, spread_ref):
    for m in range(count // 2):
        for part in range(2):
            for parity in range(2):
                at = m * LANES + part * 2 * HALF + parity * HALF
                n = 2 * m + parity
                value = sides[part * HALF : (part + 1) * HALF]
                value = powers[n : n + 1] * value if n else value
                if n < exact:
                    value, low = split(value)
                    spread_ref[count * 2 * HALF + at : count * 2 * HALF + at + HALF] = low
                spread_ref[at : at + HALF] = value.astype(jnp.bfloat16)


def coefficients(count, exact, held, unit_ref, table_ref, coarse_ref):
    tile = (PDIM, LANES)
    sign = half_sign(tile)
    group_sign = jnp.where(even_group(tile), 1.0, -1.0)
    sides = []
    for kind in range(2):
        mixed = held[kind] + group_sign * swap_groups(held[kind])
        turned = sign * roll(mixed, LANES // 2)
        sides.append((unit_ref[kind, 0] * turned, unit_ref[kind, 1] * turned, -swap_groups(mixed)))
    for o in range(3):
        plus, minus = sides[0][o], sides[1][o]
        plus_rows = (plus, -sign * roll(plus, LANES // 2))
        minus_rows = (-sign * minus, roll(minus, LANES // 2))
        for m in range(count // 2):
            lanes = slice(m * LANES, (m + 1) * LANES)
            table_plus = table_ref[0, :, lanes]
            table_minus = table_ref[1, :, lanes]
            for part in range(2):
                at = (2 * o + part) * PDIM
                value = table_plus * plus_rows[part] + table_minus * minus_rows[part]
                if 2 * m < exact:
                    value, low = split(value)
                    coarse_ref[6 * PDIM + at : 6 * PDIM + at + PDIM, lanes] = low
                    again = slice(count * 2 * HALF + m * LANES, count * 2 * HALF + (m + 1) * LANES)
                    coarse_ref[at : at + PDIM, again] = value
                coarse_ref[at : at + PDIM, lanes] = value.astype(jnp.bfloat16)


def fields(exact, coarse_ref, spread_ref, phase):
    cut = exact * 2 * HALF
    field = jnp.dot(coarse_ref[:, :cut], spread_ref[:cut], preferred_element_type=jnp.float32)
    field = field[: 6 * PDIM] + field[6 * PDIM :]
    field += jnp.dot(coarse_ref[: 6 * PDIM, cut:], spread_ref[cut:], preferred_element_type=jnp.float32)
    parts = [field[o * 2 * PDIM : (o + 1) * 2 * PDIM] for o in range(3)]
    return jnp.concatenate([jnp.sum(phase * part, axis=0, keepdims=True) for part in parts], axis=0)


def moments_kernel(
    count, exact, height, counts_ref, box_ref, positions_ref, charges_ref,
    totals_ref, decay_ref, unit_ref, before_ref, table_ref, weight_ref, phase_ref, sides_ref, powers_ref,
    spread_ref,
):
    ions = positions_ref.shape[1]
    blocks = ions // BLOCK
    pairs = count // 2
    slab_rank = lax.axis_index("slab")
    mode_rank = lax.axis_index("mode")
    box_x = jnp.full((1, 1), box_ref[0], jnp.float32)
    box_y = jnp.full((1, 1), box_ref[1], jnp.float32)
    live = counts_ref[slab_rank]
    lower_edge = slab_rank.astype(jnp.float32) * height
    scale = (2.0 * two_pi) / (box_x * box_y)

    plus, minus = table_terms(count, height, box_x, box_y)
    for m in range(pairs):
        table_ref[0, :, m * LANES : (m + 1) * LANES] = plus[m]
        table_ref[1, :, m * LANES : (m + 1) * LANES] = minus[m]

    rows = iota((8, BLOCK), 0).astype(jnp.float32)
    upward, downward = [], []
    tile = (PDIM, LANES)
    sign = half_sign(tile)
    group_sign = jnp.where(even_group(tile), 1.0, -1.0)
    found = []
    for b in range(blocks):
        span = slice(b * BLOCK, (b + 1) * BLOCK)
        x = positions_ref[0:1, span]
        y = positions_ref[1:2, span]
        t = (positions_ref[2:3, span] - lower_edge) * (2.0 / height) - 1.0
        slot = mode_rank * ions + b * BLOCK + iota((1, BLOCK), 1)
        weight = jnp.where(slot < live, charges_ref[0:1, span], 0.0)
        weight_ref[0:1, span] = weight * scale

        x8 = 8.0 * x
        y8 = 8.0 * y
        x8 = x8 - jnp.floor(x8)
        y8 = y8 - jnp.floor(y8)
        base_c, base_s = turn((rows + 1.0) * x - 0.5 * y)
        step_c, step_s = turn(rows * x8)
        phase_c, phase_s = [base_c], [base_s]
        for m in range(1, PDIM // 8):
            c, s = step_c[m : m + 1], step_s[m : m + 1]
            phase_c.append(base_c * c - base_s * s)
            phase_s.append(base_s * c + base_c * s)
        phase = jnp.concatenate(phase_c + phase_s, axis=0)
        phase_ref[b] = phase
        base_c, base_s = turn((rows + 0.5) * y)
        step_c, step_s = turn(rows * y8)
        side_c, side_s = [base_c], [base_s]
        for m in range(1, HALF // 8):
            c, s = step_c[m : m + 1], step_s[m : m + 1]
            side_c.append(base_c * c - base_s * s)
            side_s.append(base_s * c + base_c * s)
        sides = jnp.concatenate(side_c + side_s, axis=0)
        sides_ref[b] = sides

        powers = [jnp.ones_like(t), t]
        for n in range(2, count):
            powers.append(2.0 * t * powers[-1] - powers[-2])
        powers = jnp.concatenate(powers, axis=0)
        powers_ref[b] = powers
        spread(count, exact, powers, sides, spread_ref.at[b])

        heavy_high, heavy_low = split(phase * weight)
        both = jnp.concatenate([heavy_high, heavy_low], axis=0)
        across = (((1,), (1,)), ((), ()))
        cut, rest = exact * 2 * HALF, (count - exact) * 2 * HALF
        found_parts = lax.dot_general(both, spread_ref[b], across, preferred_element_type=jnp.float32)
        second = found_parts[: 2 * PDIM] + found_parts[2 * PDIM :]
        moments = second[:, :cut] + found_parts[: 2 * PDIM, cut + rest :]
        second = second[:, cut : cut + rest]
        moments = [moments[:, m * LANES : (m + 1) * LANES] for m in range(exact // 2)]
        moments += [second[:, m * LANES : (m + 1) * LANES] for m in range((count - exact) // 2)]

        sums = [jnp.zeros(tile, jnp.float32) for _ in range(4)]
        for m in range(pairs):
            piece = moments[m]
            for kind, values in enumerate((plus[m], minus[m])):
                sums[2 * kind] += values * piece[:PDIM]
                sums[2 * kind + 1] += values * piece[PDIM:]
        added = sums[0] + sign * roll(sums[1], LANES // 2)
        taken = roll(sums[3], LANES // 2) - sign * sums[2]
        found.append([swap_groups(v) + group_sign * v for v in (added, taken)])

    p, q_plus, q_minus = tile_orders()
    even = even_group(tile)
    for kind, order_q in enumerate((q_plus, q_minus)):
        wave_x, wave_y, wave_norm = wave(p, order_q, box_x, box_y)
        inverse = 1.0 / wave_norm
        unit_ref[kind, 0] = wave_x * inverse
        unit_ref[kind, 1] = wave_y * inverse
        boost = jnp.exp(wave_norm * height)
        prefix = [jnp.zeros(tile, jnp.float32)]
        for b in range(blocks):
            prefix.append(prefix[-1] + found[b][kind])
        total = prefix[-1]
        for b in range(blocks):
            before_ref[b, kind] = boost * jnp.where(even, prefix[b], total - prefix[b + 1])
        top, bottom = total[: PDIM // 2], total[PDIM // 2 :]
        small = even_group(top.shape)
        totals_ref[kind, 0] = jnp.where(small, top, roll(bottom, HALF))
        totals_ref[kind, 1] = jnp.where(small, roll(top, -HALF), bottom)
        depth = wave_norm * height
        decay_ref[kind] = jnp.where(small, depth[: PDIM // 2], depth[PDIM // 2 :])


def near_kernel(
    count, exact, chosen, before_ref, unit_ref, table_ref, phase_ref, sides_ref, powers_ref,
    forces_ref, coarse_ref, spread_ref,
):
    for i, b in enumerate(chosen):
        held = [before_ref[b, kind] for kind in range(2)]
        coefficients(count, exact, held, unit_ref, table_ref, coarse_ref.at[i])
        spread(count, exact, powers_ref[b], sides_ref[b], spread_ref.at[i])
        found = fields(exact, coarse_ref.at[i], spread_ref.at[i], phase_ref[b])
        forces_ref[:, i * BLOCK : (i + 1) * BLOCK] = found


def forces_kernel(
    count, exact, carry_ref, early_ref, late_ref, unit_ref, table_ref, weight_ref, phase_ref, sides_ref, powers_ref,
    forces_ref, coarse_ref, spread_ref,
):
    blocks = phase_ref.shape[0]
    held = []
    small = even_group((PDIM // 2, LANES))
    for kind in range(2):
        up, down = carry_ref[kind, 0], carry_ref[kind, 1]
        top = jnp.where(small, up, roll(down, HALF))
        bottom = jnp.where(small, roll(up, -HALF), down)
        held.append(jnp.concatenate([top, bottom], axis=0))
    coefficients(count, exact, held, unit_ref, table_ref, coarse_ref)
    first = early_ref.shape[1] // BLOCK
    for b in range(blocks):
        span = slice(b * BLOCK, (b + 1) * BLOCK)
        spread(count, exact, powers_ref[b], sides_ref[b], spread_ref.at[b])
        near_ref, at = (early_ref, b) if b < first else (late_ref, b - first)
        near = near_ref[:, at * BLOCK : (at + 1) * BLOCK]
        far = fields(exact, coarse_ref, spread_ref.at[b], phase_ref[b])
        forces_ref[:, span] = (far + near) * weight_ref[0:1, span]


def doublings(first, size):
    return [first << i for i in range(32) if first << i < size]


def carries(totals, decay, slabs, modes, early, late):
    slab, mode = lax.axis_index("slab"), lax.axis_index("mode")
    part = jnp.arange(2, dtype=jnp.int32)[None, :, None, None]
    depth = decay[:, None]

    def swap(value, mask):
        return lax.ppermute(value, ("slab", "mode"), [(i, i ^ mask) for i in range(slabs * modes)])

    def ahead(rank, stride):
        return part != (rank // stride) % 2

    other = swap(totals, 1)
    inside = jnp.where(ahead(mode, 1), other, 0.0)
    totals = totals + other
    strides = doublings(2, modes)
    for stride in strides[:-1]:
        other = swap(totals, stride ^ 1)
        inside = inside + jnp.where(ahead(mode, stride), other, 0.0)
        totals = totals + other
    across, both, along = [swap(totals, mask) for mask in (strides[-1] ^ 1, modes ^ strides[-1] ^ 1, modes ^ 1)]
    near = early()
    inside = inside + jnp.where(ahead(mode, strides[-1]), across, 0.0)
    totals = totals + across
    other = along + both
    outside = jnp.exp(depth) * inside
    for stride in doublings(1, slabs // 4):
        first = ahead(slab, stride)
        if stride > 1:
            other = swap(totals, (stride * modes) ^ 1)
        below = slab % stride
        steps = jnp.where(part == 0, below, stride - 1 - below).astype(jnp.float32)
        outside = outside + jnp.where(first, other * jnp.exp(-depth * steps), 0.0)
        fade = jnp.exp(-depth * float(stride))
        totals = jnp.where(first, totals + fade * other, other + fade * totals)
    totals, near = lax.optimization_barrier((totals, near))
    near = near[0], late(near[1])
    stride = slabs // 4
    group, below = slab // stride, slab % stride
    for mask in range(1, 4):
        partner = group ^ mask
        lower = partner < group
        sent = jnp.where(lower, totals[:, 1], totals[:, 0])
        other = swap(sent, (mask * stride * modes) ^ 1)[:, None]
        steps = jnp.where(lower, below, stride - 1 - below) + stride * (jnp.abs(group - partner) - 1)
        heard = other * jnp.exp(-depth * steps.astype(jnp.float32))
        outside = outside + jnp.where(part == jnp.where(lower, 0, 1), heard, 0.0)
    return outside, near


def shards(positions, charges, counts, box):
    slab_count = lax.axis_size("slab")
    mode_parts = lax.axis_size("mode")
    height = slab_span / slab_count
    count, exact = series_terms(height)
    ions = positions.shape[1]
    blocks = ions // BLOCK
    terms, all_terms = count * 2 * HALF, (count + exact) * 2 * HALF
    half = PDIM // 2
    scalar = pl.BlockSpec(memory_space=pltpu.SMEM)
    vector = pl.BlockSpec(memory_space=pltpu.VMEM)
    params = pltpu.CompilerParams(vmem_limit_bytes=40 * 1024 * 1024)
    work = [pltpu.VMEM((blocks, all_terms, BLOCK), jnp.bfloat16)]
    inputs = [
        pltpu.with_memory_space_constraint(v, pltpu.HBM) for v in (counts, box, positions, charges[None, :])
    ]
    totals, decay, *kept = pl.pallas_call(
        functools.partial(moments_kernel, count, exact, height),
        out_shape=[
            pltpu.VMEM((2, 2, half, LANES), jnp.float32),
            pltpu.VMEM((2, half, LANES), jnp.float32),
            pltpu.VMEM((2, 2, PDIM, LANES), jnp.float32),
            pltpu.VMEM((blocks, 2, PDIM, LANES), jnp.float32),
            pltpu.VMEM((2, PDIM, terms), jnp.float32),
            pltpu.VMEM((1, ions), jnp.float32),
            pltpu.VMEM((blocks, 2 * PDIM, BLOCK), jnp.float32),
            pltpu.VMEM((blocks, 2 * HALF, BLOCK), jnp.float32),
            pltpu.VMEM((blocks, count, BLOCK), jnp.float32),
        ],
        in_specs=[scalar, scalar, vector, vector],
        out_specs=[vector] * 9,
        scratch_shapes=work,
        compiler_params=params,
        name="moments",
    )(*inputs)

    fast = lambda values: [pltpu.with_memory_space_constraint(v, pltpu.VMEM) for v in values]
    unit, before, table, weight, phase, sides, powers = kept
    halves = [range(0, blocks // 2), range(blocks // 2, blocks)]

    def near(before, chosen):
        operands = fast((before, unit, table, phase, sides, powers))
        return pl.pallas_call(
            functools.partial(near_kernel, count, exact, chosen),
            out_shape=pltpu.VMEM((3, len(chosen) * BLOCK), jnp.float32),
            in_specs=[vector] * 6,
            out_specs=vector,
            scratch_shapes=[
                pltpu.VMEM((len(chosen), 12 * PDIM, all_terms), jnp.bfloat16),
                pltpu.VMEM((len(chosen), all_terms, BLOCK), jnp.bfloat16),
            ],
            compiler_params=params,
            cost_estimate=pl.CostEstimate(flops=12 * PDIM * terms * BLOCK * len(chosen) * 3 // 2, bytes_accessed=1 << 20, transcendentals=0),
            name="near",
        )(*operands)

    carry, (early, late) = carries(
        totals, decay, slab_count, mode_parts,
        lambda: (near(before, halves[0]), before), lambda held: near(held, halves[1]),
    )
    return pl.pallas_call(
        functools.partial(forces_kernel, count, exact),
        out_shape=jax.ShapeDtypeStruct((3, ions), jnp.float32),
        in_specs=[vector] * 9,
        out_specs=vector,
        scratch_shapes=[pltpu.VMEM((12 * PDIM, all_terms), jnp.bfloat16)] + work,
        compiler_params=params,
        name="forces",
    )(*fast((carry, early, late, unit, table, weight, phase, sides, powers)))


def solution(mesh):
    return jax.shard_map(
        shards,
        mesh=mesh,
        in_specs=(P(None, ("slab", "mode")), P(("slab", "mode")), P(), P()),
        out_specs=P(None, ("slab", "mode")),
        check_vma=False,
    )
```
